256 devices in a mesh: grp: 16 (over z_lo, x, core), tp: 16 (over z_hi, y).
Axes of the slice: x: 4, y: 4, z: 8 (z_hi: 4, z_lo: 2; z = z_hi * 2 + z_lo), core: 2. Of those that a mesh axis runs over, the one named last changes fastest.
Arguments:
- image: bfloat16 [32768, 1280], P(('grp', 'tp')), may hold values from -6 to 6
- text: bfloat16 [4096, 8192], P(('grp', 'tp')), may hold values from -6 to 6
- ln_gain: float32 [1280], replicated, may hold values from 0.5 to 1.5
- ln_bias: float32 [1280], replicated, may hold values from -3 to 3
- w_up: bfloat16 [1280, 5120], P(None, 'tp'), may hold values from -0.15625 to 0.15625
- b_up: float32 [5120], P('tp'), may hold values from -3 to 3
- w_down: bfloat16 [5120, 1280], P('tp'), may hold values from -0.078125 to 0.078125
- b_down: float32 [1280], replicated, may hold values from -3 to 3
- tile_count: int32 [32], P('grp'), may hold values from 1 to 4, as said below
- assign: int32 [32], P('grp'), may hold values from 0 to 1
- w_key: bfloat16 [1280, 2048], P(None, 'tp'), may hold values from -0.15625 to 0.15625
- w_value: bfloat16 [1280, 2048], P(None, 'tp'), may hold values from -0.15625 to 0.15625
- in_gain: float32 [8192], replicated, may hold values from 0.4 to 2.5
- w_query: bfloat16 [8192, 4096], P(None, 'tp'), may hold values from -0.0625 to 0.0625
- q_gain: float32 [128], replicated, may hold values from 0.25 to 1.75
- k_gain: float32 [128], replicated, may hold values from 0.4 to 2.5
- w_out: bfloat16 [4096, 8192], P('tp'), may hold values from -0.09375 to 0.09375
- attn_gate: float32 [1], replicated, may hold values from 0.4 to 1.2
- amax_hist: float32 [16, 4], replicated, may hold values from 1.5 to 4.5
Outputs:
- mixed: bfloat16 [4096, 8192], P(('grp', 'tp'))
- image_features: bfloat16 [32768, 1280], P(('grp', 'tp'))
- amax_next: float32 [16, 4], replicated
The draws below stay inside these ranges and needn't reach their ends.
Inputs may be any that keep to these rules, and one draw needn't show every extreme that they name: The first tile_count times 256 tokens of an image sample are valid.
All inputs are finite; a program needn't handle non-finite values.
Results may differ from the reference program's by a relative error of at most 0.018.
Values may be sent and summed in bfloat16 or wider, within the bound.
A program may use at most 64 MiB of HBM per device.

```python
import math
import jax
import jax.numpy as jnp
from jax import lax

ENC_D = 1280
ENC_FF = 5120
D = 8192
HD = 128
QH_DEV = 2
TILES = 4
TILE_TOK = 256
IMG_SAMP = 2
TXT_SAMP = 2
TXT_TOK = 128
HIST = 16
IMG_TOK = 1024
QH = 32
N_GRP = 16
N_TP = 16


def draw_tile_count(key, part):
    key = jax.random.fold_in(key, 7)
    counts = jax.random.randint(key, (N_GRP * IMG_SAMP,), 1, TILES + 1)
    counts = counts.at[0].set(TILES).at[1].set(1)
    return counts.astype(jnp.int32)


def with_ends(entries, stream_key, low, high):
    longest = entries.shape.index(max(entries.shape))
    spots = []
    for shift in (0, 1):
        where = [jax.random.randint(jax.random.fold_in(stream_key, axis), (), 0, length) for axis, length in enumerate(entries.shape)]
        where[longest] = (where[longest] + shift) % entries.shape[longest]
        spots.append(tuple(where))
    return entries.at[spots[0]].set(low).at[spots[1]].set(high)


def steps_of(rng, shape, shards, low, top_value):
    def one(position, parts):
        steps = jax.random.uniform(jax.random.fold_in(jax.random.fold_in(rng, 6), position), (parts,), jnp.float32, low / len(shards), top_value / len(shards))
        return jnp.repeat(jnp.exp(steps), shape[position] // parts).reshape((-1,) + (1,) * (len(shape) - position - 1))

    factor_of = one(*shards[0])
    for cut in shards[1:]:
        factor_of = factor_of * one(*cut)
    return factor_of


def gaussian(stream_key, dims, scale, bound, cuts=(), dtype=jnp.bfloat16):
    factor_of = steps_of(stream_key, dims, cuts, -0.22, 0.18) if cuts else 1.0
    array = jax.random.normal(stream_key, dims, jnp.float32) * scale * factor_of
    return jnp.minimum(jnp.maximum(array, -bound), bound).astype(dtype)


def setup_inputs(seed: int = 0) -> dict:
    seeds = jax.random.split(jax.random.key(seed), 20)
    image = gaussian(seeds[0], (N_GRP * IMG_SAMP * IMG_TOK, ENC_D), 1.0, 6.0, ((0, 256),))
    text = gaussian(seeds[1], (N_GRP * TXT_SAMP * TXT_TOK, D), 1.0, 6.0, ((0, 256),))
    ln_gain = jnp.clip(1.0 + 0.1 * jax.random.normal(seeds[2], (ENC_D,), jnp.float32), 0.5, 1.5)
    ln_bias = gaussian(seeds[3], (ENC_D,), 0.5, 3.0, (), jnp.float32)
    w_up = gaussian(seeds[4], (ENC_D, ENC_FF), ENC_D ** -0.5, 0.15625, ((1, 16),))
    b_up = gaussian(seeds[5], (ENC_FF,), 0.5, 3.0, ((0, 16),), jnp.float32)
    w_down = gaussian(seeds[6], (ENC_FF, ENC_D), ENC_FF ** -0.5, 0.078125, ((0, 16),))
    b_down = gaussian(seeds[7], (ENC_D,), 0.5, 3.0, (), jnp.float32)
    tile_count = draw_tile_count(jax.random.fold_in(seeds[19], 71), 0)
    assign = with_ends(jax.random.randint(seeds[9], (N_GRP * TXT_SAMP,), 0, IMG_SAMP), jax.random.fold_in(seeds[9], 1), 0, IMG_SAMP - 1).astype(jnp.int32)
    w_key = gaussian(seeds[10], (ENC_D, HD * N_TP), ENC_D ** -0.5, 0.15625, ((1, 16),))
    w_value = gaussian(seeds[11], (ENC_D, HD * N_TP), ENC_D ** -0.5, 0.15625, ((1, 16),))
    in_gain = jnp.clip(jnp.exp(jax.random.uniform(seeds[12], (D,), jnp.float32, math.log(0.4), math.log(2.5))), 0.4, 2.5)
    w_query = gaussian(seeds[13], (D, QH * HD), D ** -0.5, 0.0625, ((1, 16),))
    q_gain = jnp.clip(1.0 + 0.15 * jax.random.normal(seeds[14], (HD,), jnp.float32), 0.25, 1.75)
    k_gain = jnp.clip(jnp.exp(jax.random.uniform(seeds[15], (HD,), jnp.float32, math.log(0.4), math.log(2.5))), 0.4, 2.5)
    w_out = gaussian(seeds[16], (QH * HD, D), (QH * HD) ** -0.5, 0.09375, ((0, 16),))
    attn_gate = jnp.clip(jax.random.uniform(seeds[17], (1,), jnp.float32, 0.4, 1.2), 0.4, 1.2)
    amax_hist = jnp.clip(jnp.exp(jax.random.uniform(seeds[18], (HIST, 4), jnp.float32, math.log(1.5), math.log(4.5))), 1.5, 4.5)
    return dict(image=image, text=text, ln_gain=ln_gain, ln_bias=ln_bias, w_up=w_up, b_up=b_up, w_down=w_down, b_down=b_down, tile_count=tile_count, assign=assign, w_key=w_key, w_value=w_value, in_gain=in_gain, w_query=w_query, q_gain=q_gain, k_gain=k_gain, w_out=w_out, attn_gate=attn_gate, amax_hist=amax_hist)


def layer_norm(values, gain, bias):
    centre = lax.optimization_barrier(jnp.mean(values, axis=-1, keepdims=True))
    centred = values - centre
    spread = lax.optimization_barrier(jnp.mean(centred * centred, axis=-1, keepdims=True))
    return centred * lax.rsqrt(spread + 1e-05) * gain + bias

def rms_norm(values, gain, small):
    return values * lax.rsqrt(lax.optimization_barrier(jnp.mean(values * values, axis=-1, keepdims=True)) + small) * gain

def rounded(values):
    return lax.optimization_barrier(values.astype(jnp.bfloat16)).astype(jnp.float32)

def shard_sum(left, right):
    width = left.shape[1] // N_TP
    total = jnp.zeros((left.shape[0], right.shape[1]), jnp.float32)
    for shard in range(N_TP):
        product = jnp.dot(left[:, shard * width:(shard + 1) * width], right[shard * width:(shard + 1) * width], preferred_element_type=jnp.float32)
        total = total + rounded(product)
    return total

def reference(image, text, ln_gain, ln_bias, w_up, b_up, w_down, b_down, tile_count, assign, w_key, w_value, in_gain, w_query, q_gain, k_gain, w_out, attn_gate, amax_hist):
    limits = lax.optimization_barrier(jnp.max(amax_hist, axis=0))
    image_f = image.astype(jnp.float32)
    normed = layer_norm(image_f, ln_gain, ln_bias)
    cur_input = jnp.max(jnp.abs(normed))
    normed_c = jnp.clip(normed, -limits[0], limits[0]).astype(jnp.bfloat16)
    hidden = jax.nn.gelu(jnp.dot(normed_c, w_up, preferred_element_type=jnp.float32) + b_up, approximate=False)
    cur_hidden = jnp.max(jnp.abs(hidden))
    hidden_c = jnp.clip(hidden, -limits[1], limits[1]).astype(jnp.bfloat16)
    feature = image_f + shard_sum(hidden_c, w_down) + b_down
    cur_feature = jnp.max(jnp.abs(feature))
    features = jnp.clip(feature, -limits[2], limits[2]).astype(jnp.bfloat16)
    keys = jnp.dot(features, w_key, preferred_element_type=jnp.float32).reshape(-1, N_TP, HD)
    keys = rms_norm(keys, k_gain, 1e-06).astype(jnp.bfloat16).reshape(N_GRP, IMG_SAMP, IMG_TOK, N_TP, HD)
    values = jnp.dot(features, w_value, preferred_element_type=jnp.float32).astype(jnp.bfloat16).reshape(N_GRP, IMG_SAMP, IMG_TOK, N_TP, HD)
    keys = jnp.roll(keys, 1, axis=0)
    values = jnp.roll(values, 1, axis=0)
    counts = jnp.roll(tile_count.reshape(N_GRP, IMG_SAMP), 1, axis=0)
    text_f = text.astype(jnp.float32)
    tnormed = rms_norm(text_f, in_gain, 1e-05)
    cur_text = jnp.max(jnp.abs(tnormed))
    tnormed_c = jnp.clip(tnormed, -limits[3], limits[3]).astype(jnp.bfloat16)
    query = jnp.dot(tnormed_c, w_query, preferred_element_type=jnp.float32).reshape(-1, N_TP, QH_DEV, HD)
    query = rms_norm(query, q_gain, 1e-06).astype(jnp.bfloat16).reshape(N_GRP, TXT_SAMP, TXT_TOK, N_TP, QH_DEV, HD)
    chosen = assign.reshape(N_GRP, TXT_SAMP)

    def attend(group):
        group_q, group_k, group_v, group_c, group_s = group
        key_sel = group_k[group_s]
        value_sel = group_v[group_s]
        count_sel = group_c[group_s]
        scores = jnp.einsum('stnhd,sknd->snhtk', group_q.astype(jnp.float32), key_sel.astype(jnp.float32)) * HD ** (-0.5)
        valid = (jnp.arange(IMG_TOK)[None, :] < (count_sel * TILE_TOK)[:, None]).astype(jnp.float32)
        weights = jnp.exp(scores) * valid[:, None, None, None, :]
        weights = (weights / lax.optimization_barrier(jnp.sum(weights, axis=-1, keepdims=True))).astype(jnp.bfloat16)
        return jnp.einsum('snhtk,sknd->stnhd', weights.astype(jnp.float32), value_sel.astype(jnp.float32)).astype(jnp.bfloat16)
    attended = lax.map(attend, (query, keys, values, counts, chosen))
    attended = attended.reshape(N_GRP * TXT_SAMP * TXT_TOK, N_TP * QH_DEV * HD)
    total = shard_sum(attended, w_out)
    mixed = (text_f + jnp.tanh(attn_gate[0]) * total).astype(jnp.bfloat16)
    current = jnp.stack([cur_input, cur_hidden, cur_feature, cur_text])
    amax_next = jnp.concatenate([current[None, :], amax_hist[:-1]], axis=0)
    return (mixed, features, amax_next)
```

```python
import functools

import jax
import jax.numpy as jnp
from jax import lax
from jax.experimental import pallas as pl
from jax.experimental.pallas import tpu as pltpu
from jax.sharding import PartitionSpec as P

MESH = pl.DeviceIdType.MESH
BF = jnp.bfloat16
F32 = jnp.float32
TILES = 4
ROWS = 128
ENC = 1280
SH = 320
NSEM = 128


class Net:
    def __init__(self, ssem, rsem):
        self.ssem, self.rsem, self.used, self.sent = ssem, rsem, 0, []
        g, t = lax.axis_index("grp"), lax.axis_index("tp")
        self.g, self.t = g, t
        self.core, self.x, self.zl = g % 2, (g // 2) % 4, g // 8
        self.y, self.z = t % 4, t // 4

    def peer(self, axis, d):
        if axis == "y":
            return (self.g, self.z * 4 + (self.y + d) % 4)
        if axis == "z":
            return (self.g, ((self.z + d) % 4) * 4 + self.y)
        if axis == "x":
            return ((self.zl * 4 + (self.x + d) % 4) * 2 + self.core, self.t)
        if axis == "l":
            return ((self.g + 8) % 16, self.t)
        if axis == "c":
            return (self.g + 1 - 2 * self.core, self.t)
        return ((self.g + axis) % 16, ((self.z + d) % 4) * 4 + self.y)

    def barrier(self, peers):
        sem = pltpu.get_barrier_semaphore()
        for axis, d in peers:
            pl.semaphore_signal(sem, inc=1, device_id=self.peer(axis, d), device_id_type=MESH)
        pl.semaphore_wait(sem, len(peers))

    def send(self, src, dst, axis, d):
        k = self.used
        self.used += 1
        copy = pltpu.make_async_remote_copy(
            src_ref=src,
            dst_ref=dst,
            send_sem=self.ssem.at[k],
            recv_sem=self.rsem.at[k],
            device_id=self.peer(axis, d),
            device_id_type=MESH,
        )
        copy.start()
        self.sent.append(copy)
        return copy

    def finish(self):
        for copy in self.sent:
            copy.wait_send()


def rows_of(start, size, unit=16):
    return pl.ds(pl.multiple_of(start, unit), size)


def total_max(values):
    return jnp.max(jnp.max(values, axis=0, keepdims=True), axis=1, keepdims=True)


def enc_kernel(
    image, lng, lnb, bup, bdown, hist, wup, wdown,
    feat_out, cur_out,
    WU, WD, BU, NB, HB, HM, PS, RX, RY, CUR, CR, lsem, ssem, rsem,
):
    net = Net(ssem, rsem)
    x, c = net.x, net.core
    net.barrier(
        [("y", 1), ("y", 2), ("y", 3), ("z", 1), ("z", 2), ("z", 3), ("x", 1), ("x", 2), ("x", 3)]
        + [("c", 1), ("l", 1)]
    )
    own = [
        pltpu.make_async_copy(wup, WU.at[pl.ds(0, SH)], lsem.at[0]),
        pltpu.make_async_copy(wdown, WD.at[pl.ds(0, SH)], lsem.at[1]),
    ]
    for copy in own:
        copy.start()

    def mine(ref):
        return ref.at[rows_of(x * 80, 80), rows_of(c * 640, 640, 128)]

    def part(ref, slot, at):
        return ref.at[rows_of(slot * SH + at * 80, 80), rows_of(c * 640, 640, 128)]

    def half(ref, slot):
        return ref.at[pl.ds(slot * SH, SH), rows_of(c * 640, 640, 128)]

    zu = {3: net.send(mine(wup), part(WU, 3, x), "z", 1), 1: net.send(mine(wup), part(WU, 1, x), "z", 3)}
    zd = {3: net.send(mine(wdown), part(WD, 3, x), "z", 1), 1: net.send(mine(wdown), part(WD, 1, x), "z", 3)}
    BU[0] = bup[...]
    zb = [net.send(bup, BU.at[(4 - d) % 4], "z", d) for d in (1, 2, 3)]

    limits = jnp.max(hist[...], axis=0, keepdims=True)
    lim = [limits[:, i : i + 1] for i in range(4)]

    image_f = image[...].astype(F32)
    centred = image_f - jnp.mean(image_f, axis=-1, keepdims=True)
    spread = jnp.mean(centred * centred, axis=-1, keepdims=True)
    normed = centred * lax.rsqrt(spread + 1e-05) * lng[...] + lnb[...]
    cur0 = total_max(jnp.abs(normed))
    NB[0] = jnp.clip(normed, -lim[0], lim[0]).astype(BF)
    nb3 = net.send(NB.at[0], NB.at[3], "y", 1)
    nb1 = net.send(NB.at[0], NB.at[1], "y", 3)

    lo, hi = pl.ds(0, 640), pl.ds(640, 640)

    def spread_x(ref, slot):
        return (
            net.send(part(ref, slot, x), part(ref, slot, x), "x", 1),
            net.send(part(ref, slot, x), part(ref, slot, x), "x", 3),
        )

    xu, xd = {}, {}
    zu[3].wait_recv()
    zu[2] = net.send(part(WU, 3, x), part(WU, 2, x), "z", 1)
    xu[3] = spread_x(WU, 3)
    zu[1].wait_recv()
    xu[1] = spread_x(WU, 1)
    zd[1].wait_recv()
    zd[2] = net.send(part(WD, 1, x), part(WD, 2, x), "z", 3)
    xd[1] = spread_x(WD, 1)
    zd[3].wait_recv()
    xd[3] = spread_x(WD, 3)

    nb3.wait_recv()
    nb2a = net.send(NB.at[3, :, lo], NB.at[2, :, lo], "y", 1)
    nb1.wait_recv()
    nb2b = net.send(NB.at[1, :, hi], NB.at[2, :, hi], "y", 3)

    left, right = (x + 3) % 4, (x + 1) % 4
    xf = {}

    def on_u(slot):
        xu[slot][0].wait_recv()
        xf["u", slot] = net.send(part(WU, slot, left), part(WU, slot, left), "x", 1)

    def on_d(slot):
        xd[slot][1].wait_recv()
        xf["d", slot] = net.send(part(WD, slot, right), part(WD, slot, right), "x", 3)

    def core_u(slot):
        xu[slot][1].wait_recv()
        xf["u", slot].wait_recv()
        return net.send(half(WU, slot), half(WU, slot), "c", 1)

    def core_d(slot):
        xd[slot][0].wait_recv()
        xf["d", slot].wait_recv()
        return net.send(half(WD, slot), half(WD, slot), "c", 1)

    on_u(3)
    zu[2].wait_recv()
    xu[2] = spread_x(WU, 2)
    on_u(1)
    on_d(1)
    zd[2].wait_recv()
    xd[2] = spread_x(WD, 2)
    cu1 = core_u(1)
    on_d(3)
    on_u(2)
    cu3 = core_u(3)
    nb2a.wait_recv()
    nb2b.wait_recv()
    own[0].wait()
    for copy in zb:
        copy.wait_recv()
    on_d(2)
    cu2 = core_u(2)
    cu1.wait_recv()

    HM[...] = jnp.zeros_like(HM)

    def up(pair):
        rows = pl.ds(pair * 640, 640)
        bias = jnp.concatenate([BU[2 * pair][0:1, :SH], BU[2 * pair + 1][0:1, :SH]], axis=1)

        def step(i, carry):
            pre = lax.dot_general(
                NB[i], WU[rows, :], (((1,), (1,)), ((), ())), preferred_element_type=F32
            )
            pre = pre + bias
            hidden = 0.5 * pre * (1.0 + lax.erf(pre * (0.5**0.5)))
            HM[...] = jnp.maximum(HM[...], jnp.max(jnp.abs(hidden), axis=0, keepdims=True))
            HB[i, :, rows] = jnp.clip(hidden, -lim[1], lim[1]).astype(BF)
            return carry

        lax.fori_loop(0, 4, step, 0)

    up(0)
    cu2.wait_recv()
    cu3.wait_recv()
    cds = [core_d(1), core_d(3), core_d(2)]
    up(1)
    own[1].wait()
    for copy in cds:
        copy.wait_recv()

    def down(i):
        return jnp.dot(HB[i], WD[...], preferred_element_type=F32)

    PS[0] = down(2).astype(BF)
    rx0 = net.send(PS.at[0, :, lo], RX.at[0], "y", 1)
    rx1 = net.send(PS.at[0, :, hi], RX.at[1], "y", 3)
    plus = down(1)
    PS[1, :, hi] = plus[:, 640:].astype(BF)
    rx0.wait_recv()
    PS[1, :, lo] = (plus[:, :640] + RX[0].astype(F32)).astype(BF)
    ry0 = net.send(PS.at[1], RY.at[0], "y", 1)
    minus = down(3)
    PS[2, :, lo] = minus[:, :640].astype(BF)
    rx1.wait_recv()
    PS[2, :, hi] = (minus[:, 640:] + RX[1].astype(F32)).astype(BF)
    ry1 = net.send(PS.at[2], RY.at[1], "y", 3)
    feature = image[...].astype(F32) + bdown[...] + down(0)
    ry0.wait_recv()
    feature = feature + RY[0].astype(F32)
    ry1.wait_recv()
    feature = feature + RY[1].astype(F32)
    cur2 = total_max(jnp.abs(feature))
    feat_out[...] = jnp.clip(feature, -lim[2], lim[2]).astype(BF)

    cur1 = total_max(HM[...])
    lane = lax.broadcasted_iota(jnp.int32, (8, 128), 1)
    cur = jnp.where(lane == 0, cur0, 0.0) + jnp.where(lane == 1, cur1, 0.0)
    cur = cur + jnp.where(lane == 2, cur2, 0.0)
    for i, (axis, ds) in enumerate((("c", (1,)), ("y", (1, 2, 3)), ("x", (1, 2, 3)), ("z", (1, 2, 3)), ("l", (1,)))):
        CUR[i] = cur
        got = [net.send(CUR.at[i], CR.at[i, j], axis, d) for j, d in enumerate(ds)]
        for j, copy in enumerate(got):
            copy.wait_recv()
            cur = jnp.maximum(cur, CR[i, j])
    cur_out[...] = cur
    net.finish()


def encoder(image, ln_gain, ln_bias, b_up, b_down, amax_hist, w_up, w_down):
    vm = pl.BlockSpec(memory_space=pltpu.VMEM)
    hbm = pl.BlockSpec(memory_space=pl.ANY)
    bup = jnp.pad(b_up[None, :], ((0, 7), (0, 64)))
    return pl.pallas_call(
        enc_kernel,
        out_shape=(
            jax.ShapeDtypeStruct((ROWS, ENC), BF),
            jax.ShapeDtypeStruct((8, 128), F32),
        ),
        in_specs=[vm] * 6 + [hbm] * 2,
        out_specs=(vm, vm),
        scratch_shapes=[
            pltpu.VMEM((4 * SH, ENC), BF),
            pltpu.VMEM((4 * SH, ENC), BF),
            pltpu.VMEM((4, 8, 384), F32),
            pltpu.VMEM((4, ROWS, ENC), BF),
            pltpu.VMEM((4, ROWS, 4 * SH), BF),
            pltpu.VMEM((1, 640), F32),
            pltpu.VMEM((3, ROWS, ENC), BF),
            pltpu.VMEM((2, ROWS, 640), BF),
            pltpu.VMEM((2, ROWS, ENC), BF),
            pltpu.VMEM((5, 8, 128), F32),
            pltpu.VMEM((5, 3, 8, 128), F32),
            pltpu.SemaphoreType.DMA((4,)),
            pltpu.SemaphoreType.DMA((NSEM,)),
            pltpu.SemaphoreType.DMA((NSEM,)),
        ],
        compiler_params=pltpu.CompilerParams(
            collective_id=0, has_side_effects=True, vmem_limit_bytes=56 << 20
        ),
        name="encoder",
    )(image, ln_gain[None, :], ln_bias[None, :], bup, b_down[None, :], amax_hist, w_up.T, w_down)


def passed_along(value, axis, by):
    count = lax.axis_size(axis)
    return lax.ppermute(value, axis, [(i, (i + by) % count) for i in range(count)])


def rms_norm(values, gain, small):
    return values * lax.rsqrt(jnp.mean(values * values, axis=-1, keepdims=True) + small) * gain


def local(
    image,
    text,
    ln_gain,
    ln_bias,
    w_up,
    b_up,
    w_down,
    b_down,
    tile_count,
    assign,
    w_key,
    w_value,
    in_gain,
    w_query,
    q_gain,
    k_gain,
    w_out,
    attn_gate,
    amax_hist,
):
    limits = jnp.max(amax_hist, axis=0)
    head_dim = k_gain.shape[0]
    features, cur = encoder(image, ln_gain, ln_bias, b_up, b_down, amax_hist, w_up, w_down)
    moved, counts = passed_along((features, tile_count), "grp", 1)
    piece = lax.all_gather(moved, "tp", axis=0, tiled=True)
    projected = jnp.concatenate(
        [
            jnp.dot(piece, w_key, preferred_element_type=jnp.float32),
            jnp.dot(piece, w_value, preferred_element_type=jnp.float32),
        ],
        axis=1,
    )
    keys = rms_norm(projected[:, :head_dim], k_gain, 1e-06).astype(jnp.bfloat16)
    keys, values = (keys, projected[:, head_dim:].astype(jnp.bfloat16))
    img_samples = tile_count.shape[0]
    img_tokens = keys.shape[0] // img_samples
    keys = keys.reshape(img_samples, img_tokens, head_dim)
    values = values.reshape(img_samples, img_tokens, head_dim)
    text_f = text.astype(jnp.float32)
    tnormed = rms_norm(text_f, in_gain, 1e-05)
    cur_text = jnp.max(jnp.abs(tnormed))
    cur_text = lax.pmax(cur_text, ("grp", "tp"))
    tnormed_c = jnp.clip(tnormed, -limits[3], limits[3]).astype(jnp.bfloat16)
    query = jnp.dot(
        lax.all_gather(tnormed_c, "tp", axis=0, tiled=True),
        w_query,
        preferred_element_type=jnp.float32,
    )
    txt_samples = assign.shape[0]
    heads = query.shape[1] // head_dim
    query = rms_norm(query.reshape(query.shape[0], heads, head_dim), q_gain, 1e-06).astype(
        jnp.bfloat16
    )
    query = query.reshape(txt_samples, -1, heads, head_dim)
    key_sel = jnp.take(keys, assign, axis=0)
    value_sel = jnp.take(values, assign, axis=0)
    count_sel = jnp.take(counts, assign)
    scores = jnp.einsum(
        "sthd,skd->shtk", query, key_sel, preferred_element_type=jnp.float32
    ) * head_dim ** (-0.5)
    tile_tokens = img_tokens // TILES
    positions = lax.broadcasted_iota(jnp.int32, (txt_samples, img_tokens), 1)
    valid = (positions < (count_sel * tile_tokens)[:, None]).astype(jnp.float32)
    weights = jnp.exp(scores) * valid[:, None, None, :]
    weights = (weights / jnp.sum(weights, axis=-1, keepdims=True)).astype(jnp.bfloat16)
    attended = jnp.einsum(
        "shtk,skd->sthd", weights, value_sel, preferred_element_type=jnp.float32
    ).astype(jnp.bfloat16)
    attended = attended.reshape(-1, heads * head_dim)
    total = lax.psum_scatter(
        jnp.dot(attended, w_out, preferred_element_type=jnp.float32).astype(jnp.bfloat16),
        "tp",
        scatter_dimension=0,
        tiled=True,
    ).astype(jnp.float32)
    mixed = (text_f + jnp.tanh(attn_gate[0]) * total).astype(jnp.bfloat16)
    current = jnp.concatenate([cur[0, :3], cur_text[None]])
    amax_next = jnp.concatenate([current[None, :], amax_hist[:-1]], axis=0)
    return (mixed, features, amax_next)


def solution(mesh):
    rows = P(("grp", "tp"), None)
    in_specs = (
        rows, rows, P(), P(), P(None, "tp"), P("tp"), P("tp", None), P(), P("grp"), P("grp"),
        P(None, "tp"), P(None, "tp"), P(), P(None, "tp"), P(), P(), P("tp", None), P(), P(),
    )
    return jax.shard_map(local, mesh=mesh, in_specs=in_specs, out_specs=(rows, rows, P()), check_vma=False)
```

```python
import functools

import jax
import jax.numpy as jnp
from jax import lax
from jax.experimental import pallas as pl
from jax.experimental.pallas import tpu as pltpu
from jax.sharding import PartitionSpec as P

MESH = pl.DeviceIdType.MESH
BF = jnp.bfloat16
F32 = jnp.float32
D = 8192
ROWS = 128
ENC = 1280
SH = 320
NSEM = 176


class Net:
    def __init__(self, ssem, rsem):
        self.ssem, self.rsem, self.used, self.sent = ssem, rsem, 0, []
        g, t = lax.axis_index("grp"), lax.axis_index("tp")
        self.g, self.t = g, t
        self.core, self.x, self.zl = g % 2, (g // 2) % 4, g // 8
        self.y, self.z = t % 4, t // 4

    def peer(self, axis, d):
        if axis == "y":
            return (self.g, self.z * 4 + (self.y + d) % 4)
        if axis == "z":
            return (self.g, ((self.z + d) % 4) * 4 + self.y)
        if axis == "x":
            return ((self.zl * 4 + (self.x + d) % 4) * 2 + self.core, self.t)
        if axis == "l":
            return ((self.g + 8) % 16, self.t)
        if axis == "c":
            return (self.g + 1 - 2 * self.core, self.t)
        return ((self.g + axis) % 16, ((self.z + d) % 4) * 4 + self.y)

    def barrier(self, peers):
        sem = pltpu.get_barrier_semaphore()
        for axis, d in peers:
            pl.semaphore_signal(sem, inc=1, device_id=self.peer(axis, d), device_id_type=MESH)
        pl.semaphore_wait(sem, len(peers))

    def send(self, src, dst, axis, d):
        k = self.used
        self.used += 1
        copy = pltpu.make_async_remote_copy(
            src_ref=src,
            dst_ref=dst,
            send_sem=self.ssem.at[k],
            recv_sem=self.rsem.at[k],
            device_id=self.peer(axis, d),
            device_id_type=MESH,
        )
        copy.start()
        self.sent.append(copy)
        return copy

    def finish(self):
        for copy in self.sent:
            copy.wait_send()


def rows_of(start, size, unit=16):
    return pl.ds(pl.multiple_of(start, unit), size)


def total_max(values):
    return jnp.max(jnp.max(values, axis=0, keepdims=True), axis=1, keepdims=True)


def kernel(
    image, text, lng, lnb, bup, bdown, tiles, assign, ing, qg, kg, gate, hist,
    wup, wdown, wkey, wvalue, wquery, wout,
    mixed_out, feat_out, amax_out,
    WU, WD, WK, WV, WO, WQ, BU, NB, HB, HM, PF, PS, RX, RY, CUR, CR,
    T, QA, QO, QB, AS, FB, KB, VB, MK, AS2, AN, AD, AT, ADT, DN, G, OF, OS, OX, OY, FS, MX,
    lsem, ssem, rsem,
):
    net = Net(ssem, rsem)
    x, y, z, c = net.x, net.y, net.z, net.core
    net.barrier(
        [("y", 1), ("y", 2), ("y", 3), ("z", 1), ("z", 2), ("z", 3), ("x", 1), ("x", 2), ("x", 3)]
        + [("c", 1), ("l", 1)]
        + [(by, d) for by in (1, -1) for d in range(4)]
    )

    def up_part(ref, slot, at):
        return ref.at[rows_of(slot * SH + at * 80, 80), rows_of(c * 640, 640, 128)]

    def up_half(ref, slot):
        return ref.at[pl.ds(slot * SH, SH), rows_of(c * 640, 640, 128)]

    def kv_part(ref, slot, at):
        return ref.at[rows_of(c * 640 + at * 160, 160), pl.ds(slot * 128, 128)]

    def kv_half(ref, slot):
        return ref.at[rows_of(c * 640, 640), pl.ds(slot * 128, 128)]

    def wo_part(slot, at):
        return WO.at[rows_of(slot * 256 + at * 64, 64), rows_of(c * 1024, 1024, 128)]

    def wo_half(slot):
        return WO.at[pl.ds(slot * 256, 256), rows_of(c * 1024, 1024, 128)]

    left, right = (x + 3) % 4, (x + 1) % 4

    class Gather:
        def __init__(self, ref, source, part, half, forward):
            self.ref, self.part, self.half, self.forward = ref, part, half, forward
            self.zs, self.xs, self.fs, self.cs = {}, {}, {}, {}
            self.zs[3] = net.send(source, part(ref, 3, x), "z", 1)
            self.zs[1] = net.send(source, part(ref, 1, x), "z", 3)

        def z_got(self, slot):
            self.zs[slot].wait_recv()
            if slot == (3 if self.forward > 0 else 1):
                d = 1 if self.forward > 0 else 3
                self.zs[2] = net.send(self.part(self.ref, slot, x), self.part(self.ref, 2, x), "z", d)
            mine = self.part(self.ref, slot, x)
            self.xs[slot] = [net.send(mine, mine, "x", d) for d in (1, 3)]

        def x_got(self, slot):
            if self.forward > 0:
                self.xs[slot][0].wait_recv()
                other = self.part(self.ref, slot, left)
                self.fs[slot] = net.send(other, other, "x", 1)
            else:
                self.xs[slot][1].wait_recv()
                other = self.part(self.ref, slot, right)
                self.fs[slot] = net.send(other, other, "x", 3)

        def swap(self, slot):
            self.xs[slot][1 if self.forward > 0 else 0].wait_recv()
            self.fs[slot].wait_recv()
            mine = self.half(self.ref, slot)
            self.cs[slot] = net.send(mine, mine, "c", 1)

        def ready(self, *slots):
            for slot in slots:
                self.cs[slot].wait_recv()

    own = [
        pltpu.make_async_copy(wup, WU.at[pl.ds(0, SH)], lsem.at[0]),
        pltpu.make_async_copy(wdown, WD.at[pl.ds(0, SH)], lsem.at[1]),
        pltpu.make_async_copy(wkey, WK.at[:, pl.ds(0, 128)], lsem.at[2]),
        pltpu.make_async_copy(wvalue, WV.at[:, pl.ds(0, 128)], lsem.at[3]),
        pltpu.make_async_copy(
            wout.at[:, rows_of(z * 2048, 2048, 128)], WO.at[pl.ds(0, 256)], lsem.at[4]
        ),
        pltpu.make_async_copy(wquery, WQ, lsem.at[5]),
    ]
    for copy in own:
        copy.start()

    mine = (rows_of(x * 80, 80), rows_of(c * 640, 640, 128))
    gu = Gather(WU, wup.at[mine], up_part, up_half, 1)
    gd = Gather(WD, wdown.at[mine], up_part, up_half, -1)
    BU[0, 0:1, pl.ds(0, SH)] = bup[...].reshape(1, SH)
    zb = [net.send(BU.at[0], BU.at[(4 - d) % 4], "z", d) for d in (1, 2, 3)]

    limits = jnp.max(hist[...], axis=0, keepdims=True)
    lim = [limits[:, i : i + 1] for i in range(4)]

    image_f = image[...].astype(F32)
    centred = image_f - jnp.mean(image_f, axis=-1, keepdims=True)
    spread = jnp.mean(centred * centred, axis=-1, keepdims=True)
    normed = centred * lax.rsqrt(spread + 1e-05) * lng[...].reshape(1, ENC) + lnb[...].reshape(1, ENC)
    cur0 = total_max(jnp.abs(normed))
    NB[0] = jnp.clip(normed, -lim[0], lim[0]).astype(BF)
    nb3 = net.send(NB.at[0], NB.at[3], "y", 1)
    nb1 = net.send(NB.at[0], NB.at[1], "y", 3)

    text_f = text[...].astype(F32)
    tnormed = text_f * lax.rsqrt(jnp.mean(text_f * text_f, axis=-1, keepdims=True) + 1e-05)
    tnormed = tnormed * ing[...].reshape(1, D)
    cur3 = total_max(jnp.abs(tnormed))
    tlo, thi = pl.ds(0, D // 2), pl.ds(D // 2, D // 2)

    def tb(ry, zi):
        return rows_of(ry * 64 + zi * 16, 16)

    T[tb(0, z), :] = jnp.clip(tnormed, -lim[3], lim[3]).astype(BF)

    lane = lax.broadcasted_iota(jnp.int32, (8, 128), 1)
    AS[...] = jnp.where(lane == 0, assign[0], assign[1])
    sent_assign = net.send(AS, AS2, -1, 0)

    gu.z_got(3)
    gu.z_got(1)
    gd.z_got(1)
    gd.z_got(3)

    zl, zr = (z + 3) % 4, (z + 1) % 4
    tz3 = net.send(T.at[tb(0, z)], T.at[tb(0, z)], "z", 1)
    tz1 = net.send(T.at[tb(0, z)], T.at[tb(0, z)], "z", 3)

    lo, hi = pl.ds(0, 640), pl.ds(640, 640)
    nb3.wait_recv()
    nb2a = net.send(NB.at[3, :, lo], NB.at[2, :, lo], "y", 1)
    nb1.wait_recv()
    nb2b = net.send(NB.at[1, :, hi], NB.at[2, :, hi], "y", 3)

    class TextRing:
        def __init__(self, zi):
            self.zi = zi
            own_block = T.at[tb(0, zi)]
            self.a3 = net.send(own_block, T.at[tb(3, zi)], "y", 1)
            self.a1 = net.send(own_block, T.at[tb(1, zi)], "y", 3)

        def relay(self):
            self.a3.wait_recv()
            self.f = [net.send(T.at[tb(3, self.zi), tlo], T.at[tb(2, self.zi), tlo], "y", 1)]
            self.a1.wait_recv()
            self.f.append(net.send(T.at[tb(1, self.zi), thi], T.at[tb(2, self.zi), thi], "y", 3))

        def done(self):
            for copy in self.f:
                copy.wait_recv()

    rings = [TextRing(z)]

    gu.x_got(3)
    gu.z_got(2)
    gu.x_got(1)
    gd.x_got(1)
    gd.z_got(2)
    gu.swap(1)
    gd.x_got(3)
    gu.x_got(2)
    gu.swap(3)
    gk = Gather(WK, wkey.at[rows_of(c * 640 + x * 160, 160), :], kv_part, kv_half, 1)
    gv = Gather(WV, wvalue.at[rows_of(c * 640 + x * 160, 160), :], kv_part, kv_half, -1)
    rings[0].relay()
    nb2a.wait_recv()
    nb2b.wait_recv()
    own[0].wait()
    for copy in zb:
        copy.wait_recv()
    gd.x_got(2)
    gu.swap(2)
    gu.ready(1)
    gd.swap(1)
    gd.swap(3)

    HM[...] = jnp.zeros_like(HM)

    def up(pair):
        units = pl.ds(pair * 640, 640)
        bias = jnp.concatenate([BU[2 * pair][0:1, :SH], BU[2 * pair + 1][0:1, :SH]], axis=1)

        def step(i, carry):
            rows = rows_of(i * 256, 256)
            pre = lax.dot_general(
                NB[pl.ds(i * 2, 2)].reshape(256, ENC), WU[units, :], (((1,), (1,)), ((), ())),
                preferred_element_type=F32,
            )
            pre = pre + bias
            hidden = 0.5 * pre * (1.0 + lax.erf(pre * (0.5**0.5)))
            HM[...] = jnp.maximum(HM[...], jnp.max(jnp.abs(hidden), axis=0, keepdims=True))
            HB[rows, units] = jnp.clip(hidden, -lim[1], lim[1]).astype(BF)
            return carry

        lax.fori_loop(0, 2, step, 0)

    up(0)
    tz3.wait_recv()
    tz2a = net.send(T.at[tb(0, zl), tlo], T.at[tb(0, zl), tlo], "z", 1)
    rings.append(TextRing(zl))
    tz1.wait_recv()
    tz2b = net.send(T.at[tb(0, zr), thi], T.at[tb(0, zr), thi], "z", 3)
    rings.append(TextRing(zr))
    gd.swap(2)
    gu.ready(2, 3)
    up(1)
    own[1].wait()
    gd.ready(1, 2, 3)

    def down(cols):
        PF[...] = jnp.dot(HB[...], WD[:, cols], preferred_element_type=F32)

    down(lo)
    PS[0, :, lo] = PF[pl.ds(256, 128), :].astype(BF)
    rx0 = net.send(PS.at[0, :, lo], RX.at[0], "y", 1)
    PS[2, :, lo] = PF[pl.ds(384, 128), :].astype(BF)
    OWN0 = image[:, lo].astype(F32) + bdown[lo].reshape(1, 640) + PF[pl.ds(0, 128), :]
    plus_lo = PF[pl.ds(128, 128), :]
    down(hi)
    PS[0, :, hi] = PF[pl.ds(256, 128), :].astype(BF)
    rx1 = net.send(PS.at[0, :, hi], RX.at[1], "y", 3)
    PS[1, :, hi] = PF[pl.ds(128, 128), :].astype(BF)
    rx0.wait_recv()
    PS[1, :, lo] = (plus_lo + RX[0].astype(F32)).astype(BF)
    ry0 = net.send(PS.at[1], RY.at[0], "y", 1)
    rx1.wait_recv()
    PS[2, :, hi] = (PF[pl.ds(384, 128), :] + RX[1].astype(F32)).astype(BF)
    ry1 = net.send(PS.at[2], RY.at[1], "y", 3)

    rings[1].relay()
    rings[2].relay()
    tz2a.wait_recv()
    tz2b.wait_recv()
    zo = (z + 2) % 4
    rings.append(TextRing(zo))
    for part in (gk, gv):
        part.z_got(3)
        part.z_got(1)
    wo_zs = {}
    for d in (1, 3, 2):
        cut = rows_of(((z + d) % 4) * 2048 + c * 1024, 1024, 128)
        wo_zs[4 - d] = net.send(wout.at[rows_of(x * 64, 64), cut], wo_part(4 - d, x), "z", d)

    ry0.wait_recv()
    ry1.wait_recv()
    feat_lo = OWN0 + RY[0, :, lo].astype(F32) + RY[1, :, lo].astype(F32)
    feat_hi = image[:, hi].astype(F32) + bdown[hi].reshape(1, 640) + PF[pl.ds(0, 128), :]
    feat_hi = feat_hi + RY[0, :, hi].astype(F32) + RY[1, :, hi].astype(F32)
    cur2 = jnp.maximum(total_max(jnp.abs(feat_lo)), total_max(jnp.abs(feat_hi)))
    FB[0, :, lo] = jnp.clip(feat_lo, -lim[2], lim[2]).astype(BF)
    FB[0, :, hi] = jnp.clip(feat_hi, -lim[2], lim[2]).astype(BF)
    fb3 = net.send(FB.at[0], FB.at[3], "y", 1)
    fb1 = net.send(FB.at[0], FB.at[1], "y", 3)
    feat_out[...] = FB[0]

    cur1 = total_max(HM[...])
    cur = jnp.where(lane == 0, cur0, 0.0) + jnp.where(lane == 1, cur1, 0.0)
    cur = cur + jnp.where(lane == 2, cur2, 0.0) + jnp.where(lane == 3, cur3, 0.0)
    CUR[0] = cur
    stages = (("c", (1,)), ("y", (1, 2, 3)), ("x", (1, 2, 3)), ("z", (1, 2, 3)), ("l", (1,)))

    def max_send(i):
        axis, ds = stages[i]
        return [net.send(CUR.at[i], CR.at[i, j], axis, d) for j, d in enumerate(ds)]

    def max_take(i, copies):
        value = CUR[i]
        for j, copy in enumerate(copies):
            copy.wait_recv()
            value = jnp.maximum(value, CR[i, j])
        CUR[i + 1] = value

    going = max_send(0)

    for part in (gk, gv):
        part.z_got(2)
        part.x_got(3)
        part.x_got(1)

    fb3.wait_recv()
    fb2a = net.send(FB.at[3, :, lo], FB.at[2, :, lo], "y", 1)
    fb1.wait_recv()
    fb2b = net.send(FB.at[1, :, hi], FB.at[2, :, hi], "y", 3)
    max_take(0, going)
    going = max_send(1)

    for part in (gk, gv):
        part.x_got(2)
        part.swap(1)
        part.swap(3)

    rings[3].relay()
    for ring in rings:
        ring.done()
    own[5].wait()
    QA[...] = jnp.zeros_like(QA)

    def query_step(i, carry):
        span = rows_of(i * 1024, 1024, 128)
        QA[...] += jnp.dot(T[:, span], WQ[span, :], preferred_element_type=F32)
        return carry

    lax.fori_loop(0, D // 1024, query_step, 0)
    for h in range(2):
        cols = pl.ds(h * 128, 128)
        q = QA[:, cols]
        q = q * lax.rsqrt(jnp.mean(q * q, axis=-1, keepdims=True) + 1e-06) * qg[...].reshape(1, 128)
        QO[:, cols] = q.astype(BF)
    qs = [net.send(QO, QB.at[(4 - d) % 4], -1, d) for d in range(4)]

    wo_xs, wo_fs, wo_cs = {}, {}, {}
    for slot in (3, 1, 2):
        wo_zs[slot].wait_recv()
        wo_xs[slot] = [net.send(wo_part(slot, x), wo_part(slot, x), "x", d) for d in (1, 3)]

    for part in (gk, gv):
        part.swap(2)
    own[2].wait()
    own[3].wait()
    for part in (gk, gv):
        part.ready(1, 2, 3)
    fb2a.wait_recv()
    fb2b.wait_recv()

    rows_f = FB[...].reshape(512, ENC)
    keys = jnp.dot(rows_f, WK[...], preferred_element_type=F32)
    for r in range(4):
        k = keys[:, r * 128 : (r + 1) * 128]
        k = k * lax.rsqrt(jnp.mean(k * k, axis=-1, keepdims=True) + 1e-06) * kg[...].reshape(1, 128)
        KB[r] = k.astype(BF)
    values = jnp.dot(rows_f, WV[...], preferred_element_type=F32)
    for r in range(4):
        VB[r, :, pl.ds(0, 128)] = values[:, r * 128 : (r + 1) * 128].astype(BF)
        VB[r, :, pl.ds(128, 128)] = jnp.ones((512, 128), BF)

    max_take(1, going)
    going = max_send(2)

    sent_assign.wait_recv()
    count = jnp.where(z < 2, tiles[0], tiles[1]) * 256
    col = lax.broadcasted_iota(jnp.int32, (256, 512), 1)
    row = lax.broadcasted_iota(jnp.int32, (256, 512), 0)
    at = ((z % 2) * 4 + ((y + (col >> 7)) & 3)) * 128 + (col & 127)
    chosen = jnp.where((row & 63) < 32, AS2[0:1, 0:1], AS2[0:1, 1:2])
    MK[...] = jnp.where((at < count) & (chosen == z // 2), 1.0, 0.0)

    for copy in qs:
        copy.wait_recv()
    ats = []
    lane_w = lax.broadcasted_iota(jnp.int32, (256, 128), 1)
    for r in (2, 1, 3, 0):
        dens = []
        for h in range(2):
            cols = pl.ds(h * 128, 128)
            scores = lax.dot_general(
                QB[r, :, cols], KB[r], (((1,), (1,)), ((), ())), preferred_element_type=F32
            )
            weights = (jnp.exp(scores * (128**-0.5)) * MK[...]).astype(BF)
            both = jnp.dot(weights, VB[r], preferred_element_type=F32)
            AN[r, :, cols] = both[:, :128].astype(BF)
            dens.append(both[:, 128:])
        packed = jnp.where(lane_w == 0, dens[0], jnp.where(lane_w == 1, dens[1], 0.0))
        AD[r] = packed.T[0:8, :]
        ats.append(net.send(AN.at[r], AT.at[(4 - r) % 4], 1, r))
        ats.append(net.send(AD.at[r], ADT.at[(4 - r) % 4], 1, r))

    for slot in (3, 1, 2):
        if slot == 1:
            wo_xs[slot][1].wait_recv()
            wo_fs[slot] = net.send(wo_part(slot, right), wo_part(slot, right), "x", 3)
        else:
            wo_xs[slot][0].wait_recv()
            wo_fs[slot] = net.send(wo_part(slot, left), wo_part(slot, left), "x", 1)
    for slot in (3, 1, 2):
        wo_xs[slot][0 if slot == 1 else 1].wait_recv()
        wo_fs[slot].wait_recv()
        wo_cs[slot] = net.send(wo_half(slot), wo_half(slot), "c", 1)

    max_take(2, going)
    going = max_send(3)

    for copy in ats:
        copy.wait_recv()
    DN[...] = jnp.ones_like(DN)
    DN[pl.ds(0, 8), :] = ADT[0] + ADT[1] + ADT[2] + ADT[3]
    den = DN[...].T
    for h in range(2):
        cols = pl.ds(h * 128, 128)
        num = AT[0, :, cols].astype(F32) + AT[1, :, cols].astype(F32)
        num = num + AT[2, :, cols].astype(F32) + AT[3, :, cols].astype(F32)
        G[:, cols] = (num / den[:, h : h + 1]).astype(BF)
    gs = [net.send(G.at[:, pl.ds(0, 256)], G.at[:, pl.ds((4 - d) * 256, 256)], "z", d) for d in (1, 3, 2)]

    own[4].wait()
    for slot in (1, 2, 3):
        wo_cs[slot].wait_recv()
    for copy in gs:
        copy.wait_recv()

    olo, ohi = pl.ds(0, 1024), pl.ds(1024, 1024)
    OF[...] = jnp.dot(G[...], WO[:, olo], preferred_element_type=F32)
    OS[0, :, olo] = OF[pl.ds(128, 64), :].astype(BF)
    ox0 = net.send(OS.at[0, :, olo], OX.at[0], "y", 1)
    OS[2, :, olo] = OF[pl.ds(192, 64), :].astype(BF)
    out_lo = OF[pl.ds(0, 64), :]
    oplus = OF[pl.ds(64, 64), :]
    OF[...] = jnp.dot(G[...], WO[:, ohi], preferred_element_type=F32)
    OS[0, :, ohi] = OF[pl.ds(128, 64), :].astype(BF)
    ox1 = net.send(OS.at[0, :, ohi], OX.at[1], "y", 3)
    OS[1, :, ohi] = OF[pl.ds(64, 64), :].astype(BF)
    ox0.wait_recv()
    OS[1, :, olo] = (oplus + OX[0].astype(F32)).astype(BF)
    oy0 = net.send(OS.at[1], OY.at[0], "y", 1)
    ox1.wait_recv()
    OS[2, :, ohi] = (OF[pl.ds(192, 64), :] + OX[1].astype(F32)).astype(BF)
    oy1 = net.send(OS.at[2], OY.at[1], "y", 3)
    max_take(3, going)
    going = max_send(4)
    oy0.wait_recv()
    oy1.wait_recv()
    FS[:, olo] = (out_lo + OY[0, :, olo].astype(F32) + OY[1, :, olo].astype(F32)).astype(BF)
    FS[:, ohi] = (OF[pl.ds(0, 64), :] + OY[0, :, ohi].astype(F32) + OY[1, :, ohi].astype(F32)).astype(BF)
    fs = {}
    for d in (2, 1, 3):
        fs[4 - d] = net.send(FS.at[rows_of(((z + d) % 4) * 16, 16)], MX.at[4 - d], "z", d)
    max_take(4, going)
    amax_out[0:1, :] = CUR[5][0:1, 0:4]
    amax_out[pl.ds(1, 15), :] = hist[pl.ds(0, 15), :]
    strength = jnp.tanh(jnp.full((1, 128), gate[0], F32))[:, 0:1]
    for r in (0, 1, 3, 2):
        cols = rows_of(((z + r) % 4) * 2048, 2048, 128)
        if r:
            fs[r].wait_recv()
            total = MX[r].astype(F32)
        else:
            total = FS[rows_of(z * 16, 16), :].astype(F32)
        mixed_out[:, cols] = (text[:, cols].astype(F32) + strength * total).astype(BF)
    net.finish()


def local(
    image, text, ln_gain, ln_bias, w_up, b_up, w_down, b_down, tile_count, assign,
    w_key, w_value, in_gain, w_query, q_gain, k_gain, w_out, attn_gate, amax_hist,
):
    vm = pl.BlockSpec(memory_space=pltpu.VMEM)
    sm = pl.BlockSpec(memory_space=pltpu.SMEM)
    hbm = pl.BlockSpec(memory_space=pl.ANY)
    return pl.pallas_call(
        kernel,
        out_shape=(
            jax.ShapeDtypeStruct((16, D), BF),
            jax.ShapeDtypeStruct((ROWS, ENC), BF),
            jax.ShapeDtypeStruct((16, 4), F32),
        ),
        in_specs=[vm] * 6 + [sm] * 2 + [vm] * 3 + [sm, vm] + [hbm] * 6,
        out_specs=(vm, vm, vm),
        scratch_shapes=[
            pltpu.VMEM((4 * SH, ENC), BF),
            pltpu.VMEM((4 * SH, ENC), BF),
            pltpu.VMEM((ENC, 512), BF),
            pltpu.VMEM((ENC, 512), BF),
            pltpu.VMEM((1024, 2048), BF),
            pltpu.VMEM((D, 256), BF),
            pltpu.VMEM((4, 8, 384), F32),
            pltpu.VMEM((4, ROWS, ENC), BF),
            pltpu.VMEM((512, 4 * SH), BF),
            pltpu.VMEM((1, 640), F32),
            pltpu.VMEM((512, 640), F32),
            pltpu.VMEM((3, ROWS, ENC), BF),
            pltpu.VMEM((2, ROWS, 640), BF),
            pltpu.VMEM((2, ROWS, ENC), BF),
            pltpu.VMEM((6, 8, 128), F32),
            pltpu.VMEM((5, 3, 8, 128), F32),
            pltpu.VMEM((256, D), BF),
            pltpu.VMEM((256, 256), F32),
            pltpu.VMEM((256, 256), BF),
            pltpu.VMEM((4, 256, 256), BF),
            pltpu.VMEM((8, 128), jnp.int32),
            pltpu.VMEM((4, ROWS, ENC), BF),
            pltpu.VMEM((4, 512, 128), BF),
            pltpu.VMEM((4, 512, 256), BF),
            pltpu.VMEM((256, 512), F32),
            pltpu.VMEM((8, 128), jnp.int32),
            pltpu.VMEM((4, 256, 256), BF),
            pltpu.VMEM((4, 8, 256), F32),
            pltpu.VMEM((4, 256, 256), BF),
            pltpu.VMEM((4, 8, 256), F32),
            pltpu.VMEM((128, 256), F32),
            pltpu.VMEM((256, 1024), BF),
            pltpu.VMEM((256, 1024), F32),
            pltpu.VMEM((3, 64, 2048), BF),
            pltpu.VMEM((2, 64, 1024), BF),
            pltpu.VMEM((2, 64, 2048), BF),
            pltpu.VMEM((64, 2048), BF),
            pltpu.VMEM((4, 16, 2048), BF),
            pltpu.SemaphoreType.DMA((8,)),
            pltpu.SemaphoreType.DMA((NSEM,)),
            pltpu.SemaphoreType.DMA((NSEM,)),
        ],
        compiler_params=pltpu.CompilerParams(
            collective_id=0, has_side_effects=True, vmem_limit_bytes=60 << 20
        ),
        name="block",
    )(
        image, text, ln_gain, ln_bias, b_up, b_down, tile_count, assign, in_gain, q_gain, k_gain,
        attn_gate, amax_hist, w_up.T, w_down, w_key, w_value, w_query, w_out,
    )


def solution(mesh):
    rows = P(("grp", "tp"), None)
    in_specs = (
        rows, rows, P(), P(), P(None, "tp"), P("tp"), P("tp", None), P(), P("grp"), P("grp"),
        P(None, "tp"), P(None, "tp"), P(), P(None, "tp"), P(), P(), P("tp", None), P(), P(),
    )
    return jax.shard_map(local, mesh=mesh, in_specs=in_specs, out_specs=(rows, rows, P()), check_vma=False)
```

```python
import functools

import jax
import jax.numpy as jnp
from jax import lax
from jax.experimental import pallas as pl
from jax.experimental.pallas import tpu as pltpu
from jax.sharding import PartitionSpec as P

MESH = pl.DeviceIdType.MESH
BF = jnp.bfloat16
F32 = jnp.float32
D = 8192
ROWS = 128
ENC = 1280
SH = 320
NSEM = 160


class Net:
    def __init__(self, ssem, rsem):
        self.ssem, self.rsem, self.used, self.sent = ssem, rsem, 0, []
        g, t = lax.axis_index("grp"), lax.axis_index("tp")
        self.g, self.t = g, t
        self.core, self.x, self.zl = g % 2, (g // 2) % 4, g // 8
        self.y, self.z = t % 4, t // 4

    def peer(self, axis, d):
        if axis == "y":
            return (self.g, self.z * 4 + (self.y + d) % 4)
        if axis == "z":
            return (self.g, ((self.z + d) % 4) * 4 + self.y)
        if axis == "x":
            return ((self.zl * 4 + (self.x + d) % 4) * 2 + self.core, self.t)
        if axis == "l":
            return ((self.g + 8) % 16, self.t)
        if axis == "c":
            return (self.g + 1 - 2 * self.core, self.t)
        return ((self.g + axis) % 16, ((self.z + d) % 4) * 4 + self.y)

    def barrier(self, peers):
        sem = pltpu.get_barrier_semaphore()
        for axis, d in peers:
            pl.semaphore_signal(sem, inc=1, device_id=self.peer(axis, d), device_id_type=MESH)
        pl.semaphore_wait(sem, len(peers))

    def send(self, src, dst, axis, d):
        k = self.used
        self.used += 1
        copy = pltpu.make_async_remote_copy(
            src_ref=src,
            dst_ref=dst,
            send_sem=self.ssem.at[k],
            recv_sem=self.rsem.at[k],
            device_id=self.peer(axis, d),
            device_id_type=MESH,
        )
        copy.start()
        self.sent.append(copy)
        return copy

    def finish(self):
        for copy in self.sent:
            copy.wait_send()


def rows_of(start, size, unit=16):
    return pl.ds(pl.multiple_of(start, unit), size)


def total_max(values):
    return jnp.max(jnp.max(values, axis=0, keepdims=True), axis=1, keepdims=True)


def kernel(
    image, text, lng, lnb, bup, bdown, tiles, assign, ing, qg, kg, gate, hist,
    wup, wdown, wkey, wvalue, wquery, wout,
    mixed_out, feat_out, amax_out,
    WU, WD, WK, WV, WO, WQ, BU, NB, HB, HM, PF, PS, RX, RY, CUR, CR,
    T, QA, QO, QB, AS, FB, KB, VB, MK, AS2, AN, AD, AT, ADT, DN, G, OF, OS, OX, OY, FS, MX,
    lsem, ssem, rsem,
):
    net = Net(ssem, rsem)
    x, y, z, c = net.x, net.y, net.z, net.core
    net.barrier(
        [("y", 1), ("y", 2), ("y", 3), ("z", 1), ("z", 2), ("z", 3), ("x", 1), ("x", 2), ("x", 3)]
        + [("c", 1), ("l", 1)]
        + [(by, d) for by in (1, -1) for d in range(4)]
    )

    def up_part(ref, slot, at):
        return ref.at[rows_of(slot * SH + at * 80, 80), rows_of(c * 640, 640, 128)]

    def up_half(ref, slot):
        return ref.at[pl.ds(slot * SH, SH), rows_of(c * 640, 640, 128)]

    def kv_part(ref, slot, at):
        return ref.at[rows_of(c * 640 + at * 160, 160), pl.ds(slot * 128, 128)]

    def kv_half(ref, slot):
        return ref.at[rows_of(c * 640, 640), pl.ds(slot * 128, 128)]

    def wo_part(slot, at):
        return WO.at[rows_of(slot * 256 + at * 64, 64), rows_of(c * 1024, 1024, 128)]

    def wo_half(slot):
        return WO.at[pl.ds(slot * 256, 256), rows_of(c * 1024, 1024, 128)]

    left, right = (x + 3) % 4, (x + 1) % 4

    class Gather:
        def __init__(self, ref, source, part, half, forward):
            self.ref, self.part, self.half, self.forward = ref, part, half, forward
            self.zs, self.xs, self.fs, self.cs = {}, {}, {}, {}
            self.zs[3] = net.send(source, part(ref, 3, x), "z", 1)
            self.zs[1] = net.send(source, part(ref, 1, x), "z", 3)

        def z_got(self, slot):
            self.zs[slot].wait_recv()
            if slot == (3 if self.forward > 0 else 1):
                d = 1 if self.forward > 0 else 3
                self.zs[2] = net.send(self.part(self.ref, slot, x), self.part(self.ref, 2, x), "z", d)
            mine = self.part(self.ref, slot, x)
            self.xs[slot] = [net.send(mine, mine, "x", d) for d in (1, 3)]

        def x_got(self, slot):
            if self.forward > 0:
                self.xs[slot][0].wait_recv()
                other = self.part(self.ref, slot, left)
                self.fs[slot] = net.send(other, other, "x", 1)
            else:
                self.xs[slot][1].wait_recv()
                other = self.part(self.ref, slot, right)
                self.fs[slot] = net.send(other, other, "x", 3)

        def swap(self, slot):
            self.xs[slot][1 if self.forward > 0 else 0].wait_recv()
            self.fs[slot].wait_recv()
            mine = self.half(self.ref, slot)
            self.cs[slot] = net.send(mine, mine, "c", 1)

        def ready(self, *slots):
            for slot in slots:
                self.cs[slot].wait_recv()

    own = [
        pltpu.make_async_copy(wup, WU.at[pl.ds(0, SH)], lsem.at[0]),
        pltpu.make_async_copy(wdown, WD.at[pl.ds(0, SH)], lsem.at[1]),
        pltpu.make_async_copy(wkey, WK.at[:, pl.ds(0, 128)], lsem.at[2]),
        pltpu.make_async_copy(wvalue, WV.at[:, pl.ds(0, 128)], lsem.at[3]),
        pltpu.make_async_copy(
            wout.at[:, rows_of(z * 2048, 2048, 128)], WO.at[pl.ds(0, 256)], lsem.at[4]
        ),
        pltpu.make_async_copy(wquery, WQ, lsem.at[5]),
    ]
    for copy in own:
        copy.start()

    mine = (rows_of(x * 80, 80), rows_of(c * 640, 640, 128))
    gu = Gather(WU, wup.at[mine], up_part, up_half, 1)
    gd = Gather(WD, wdown.at[mine], up_part, up_half, -1)
    BU[0, 0:1, pl.ds(0, SH)] = bup[...].reshape(1, SH)
    zb = [net.send(BU.at[0], BU.at[(4 - d) % 4], "z", d) for d in (1, 2, 3)]

    limits = jnp.max(hist[...], axis=1, keepdims=True)
    lim = [limits[i : i + 1, :] for i in range(4)]

    image_f = image[...].astype(F32)
    centred = image_f - jnp.mean(image_f, axis=-1, keepdims=True)
    spread = jnp.mean(centred * centred, axis=-1, keepdims=True)
    normed = centred * lax.rsqrt(spread + 1e-05) * lng[...].reshape(1, ENC) + lnb[...].reshape(1, ENC)
    cur0 = total_max(jnp.abs(normed))
    NB[0] = jnp.clip(normed, -lim[0], lim[0]).astype(BF)
    nb3 = net.send(NB.at[0], NB.at[3], "y", 1)
    nb1 = net.send(NB.at[0], NB.at[1], "y", 3)

    text_f = text[...].astype(F32)
    tnormed = text_f * lax.rsqrt(jnp.mean(text_f * text_f, axis=-1, keepdims=True) + 1e-05)
    tnormed = tnormed * ing[...].reshape(1, D)
    cur3 = total_max(jnp.abs(tnormed))
    tlo, thi = pl.ds(0, D // 2), pl.ds(D // 2, D // 2)

    def tb(ry, zi):
        return rows_of(ry * 64 + zi * 16, 16)

    T[tb(0, z), :] = jnp.clip(tnormed, -lim[3], lim[3]).astype(BF)

    lane = lax.broadcasted_iota(jnp.int32, (8, 128), 1)
    AS[...] = jnp.where(lane == 0, assign[0], assign[1])
    sent_assign = net.send(AS, AS2, -1, 0)

    gu.z_got(3)
    gu.z_got(1)
    gd.z_got(1)
    gd.z_got(3)

    zl, zr = (z + 3) % 4, (z + 1) % 4
    tz3 = net.send(T.at[tb(0, z)], T.at[tb(0, z)], "z", 1)
    tz1 = net.send(T.at[tb(0, z)], T.at[tb(0, z)], "z", 3)

    lo, hi = pl.ds(0, 640), pl.ds(640, 640)
    nb3.wait_recv()
    nb2a = net.send(NB.at[3, :, lo], NB.at[2, :, lo], "y", 1)
    nb1.wait_recv()
    nb2b = net.send(NB.at[1, :, hi], NB.at[2, :, hi], "y", 3)

    class TextRing:
        def __init__(self, zi):
            self.zi = zi
            own_block = T.at[tb(0, zi)]
            self.a3 = net.send(own_block, T.at[tb(3, zi)], "y", 1)
            self.a1 = net.send(own_block, T.at[tb(1, zi)], "y", 3)

        def relay(self):
            self.a3.wait_recv()
            self.f = [net.send(T.at[tb(3, self.zi), tlo], T.at[tb(2, self.zi), tlo], "y", 1)]
            self.a1.wait_recv()
            self.f.append(net.send(T.at[tb(1, self.zi), thi], T.at[tb(2, self.zi), thi], "y", 3))

        def done(self):
            for copy in self.f:
                copy.wait_recv()

    rings = [TextRing(z)]

    gu.x_got(3)
    gu.z_got(2)
    gu.x_got(1)
    gd.x_got(1)
    gd.z_got(2)
    gu.swap(1)
    gd.x_got(3)
    gu.x_got(2)
    gu.swap(3)
    gk = Gather(WK, wkey.at[rows_of(c * 640 + x * 160, 160), :], kv_part, kv_half, 1)
    gv = Gather(WV, wvalue.at[rows_of(c * 640 + x * 160, 160), :], kv_part, kv_half, -1)
    rings[0].relay()
    nb2a.wait_recv()
    nb2b.wait_recv()
    own[0].wait()
    for copy in zb:
        copy.wait_recv()
    gd.x_got(2)
    gu.swap(2)
    gu.ready(1)
    gd.swap(1)
    gd.swap(3)

    HM[...] = jnp.zeros_like(HM)

    def up(pair):
        units = pl.ds(pair * 640, 640)
        bias = jnp.concatenate([BU[2 * pair][0:1, :SH], BU[2 * pair + 1][0:1, :SH]], axis=1)

        def step(i, carry):
            rows = rows_of(i * 256, 256)
            pre = lax.dot_general(
                NB[pl.ds(i * 2, 2)].reshape(256, ENC), WU[units, :], (((1,), (1,)), ((), ())),
                preferred_element_type=F32,
            )
            pre = pre + bias
            hidden = 0.5 * pre * (1.0 + lax.erf(pre * (0.5**0.5)))
            HM[...] = jnp.maximum(HM[...], jnp.max(jnp.abs(hidden), axis=0, keepdims=True))
            HB[rows, units] = jnp.clip(hidden, -lim[1], lim[1]).astype(BF)
            return carry

        lax.fori_loop(0, 2, step, 0)

    up(0)
    tz3.wait_recv()
    tz2a = net.send(T.at[tb(0, zl), tlo], T.at[tb(0, zl), tlo], "z", 1)
    rings.append(TextRing(zl))
    tz1.wait_recv()
    tz2b = net.send(T.at[tb(0, zr), thi], T.at[tb(0, zr), thi], "z", 3)
    rings.append(TextRing(zr))
    gd.swap(2)
    gu.ready(2, 3)
    up(1)
    own[1].wait()
    gd.ready(1, 2, 3)

    def down(cols):
        PF[...] = jnp.dot(HB[...], WD[:, cols], preferred_element_type=F32)

    down(lo)
    PS[0, :, lo] = PF[pl.ds(256, 128), :].astype(BF)
    rx0 = net.send(PS.at[0, :, lo], RX.at[0], "y", 1)
    PS[2, :, lo] = PF[pl.ds(384, 128), :].astype(BF)
    OWN0 = image[:, lo].astype(F32) + bdown[lo].reshape(1, 640) + PF[pl.ds(0, 128), :]
    plus_lo = PF[pl.ds(128, 128), :]
    down(hi)
    PS[0, :, hi] = PF[pl.ds(256, 128), :].astype(BF)
    rx1 = net.send(PS.at[0, :, hi], RX.at[1], "y", 3)
    PS[1, :, hi] = PF[pl.ds(128, 128), :].astype(BF)
    rx0.wait_recv()
    PS[1, :, lo] = (plus_lo + RX[0].astype(F32)).astype(BF)
    ry0 = net.send(PS.at[1], RY.at[0], "y", 1)
    rx1.wait_recv()
    PS[2, :, hi] = (PF[pl.ds(384, 128), :] + RX[1].astype(F32)).astype(BF)
    ry1 = net.send(PS.at[2], RY.at[1], "y", 3)

    rings[1].relay()
    rings[2].relay()
    tz2a.wait_recv()
    tz2b.wait_recv()
    zo = (z + 2) % 4
    rings.append(TextRing(zo))
    for part in (gk, gv):
        part.z_got(3)
        part.z_got(1)
    wo_zs = {}
    for d in (1, 3, 2):
        cut = rows_of(((z + d) % 4) * 2048 + c * 1024, 1024, 128)
        wo_zs[4 - d] = net.send(wout.at[rows_of(x * 64, 64), cut], wo_part(4 - d, x), "z", d)

    ry0.wait_recv()
    ry1.wait_recv()
    feat_lo = OWN0 + RY[0, :, lo].astype(F32) + RY[1, :, lo].astype(F32)
    feat_hi = image[:, hi].astype(F32) + bdown[hi].reshape(1, 640) + PF[pl.ds(0, 128), :]
    feat_hi = feat_hi + RY[0, :, hi].astype(F32) + RY[1, :, hi].astype(F32)
    cur2 = jnp.maximum(total_max(jnp.abs(feat_lo)), total_max(jnp.abs(feat_hi)))
    FB[0, :, lo] = jnp.clip(feat_lo, -lim[2], lim[2]).astype(BF)
    FB[0, :, hi] = jnp.clip(feat_hi, -lim[2], lim[2]).astype(BF)
    fb3 = net.send(FB.at[0], FB.at[3], "y", 1)
    fb1 = net.send(FB.at[0], FB.at[1], "y", 3)
    feat_out[...] = FB[0]

    cur1 = total_max(HM[...])
    line = lax.broadcasted_iota(jnp.int32, (8, 128), 0)
    cur = jnp.where(line == 0, cur0, 0.0) + jnp.where(line == 1, cur1, 0.0)
    cur = cur + jnp.where(line == 2, cur2, 0.0) + jnp.where(line == 3, cur3, 0.0)
    CUR[0] = cur
    stages = (("c", (1,)), ("y", (1, 2, 3)), ("x", (1, 2, 3)), ("z", (1, 2, 3)), ("l", (1,)))

    def max_send(i):
        axis, ds = stages[i]
        return [net.send(CUR.at[i], CR.at[i, j], axis, d) for j, d in enumerate(ds)]

    def max_take(i, copies):
        value = CUR[i]
        for j, copy in enumerate(copies):
            copy.wait_recv()
            value = jnp.maximum(value, CR[i, j])
        CUR[i + 1] = value

    going = max_send(0)

    for part in (gk, gv):
        part.z_got(2)
        part.x_got(3)
        part.x_got(1)

    fb3.wait_recv()
    fb2a = net.send(FB.at[3, :, lo], FB.at[2, :, lo], "y", 1)
    fb1.wait_recv()
    fb2b = net.send(FB.at[1, :, hi], FB.at[2, :, hi], "y", 3)
    max_take(0, going)
    going = max_send(1)

    for part in (gk, gv):
        part.x_got(2)
        part.swap(1)
        part.swap(3)

    rings[3].relay()
    for ring in rings:
        ring.done()
    own[5].wait()
    QA[...] = jnp.zeros_like(QA)

    def query_step(i, carry):
        span = rows_of(i * 1024, 1024, 128)
        QA[...] += jnp.dot(T[:, span], WQ[span, :], preferred_element_type=F32)
        return carry

    lax.fori_loop(0, D // 1024, query_step, 0)
    for h in range(2):
        cols = pl.ds(h * 128, 128)
        q = QA[:, cols]
        q = q * lax.rsqrt(jnp.mean(q * q, axis=-1, keepdims=True) + 1e-06) * qg[...].reshape(1, 128)
        QO[:, cols] = q.astype(BF)
    qs = [net.send(QO, QB.at[(4 - d) % 4], -1, d) for d in range(4)]

    wo_xs, wo_fs, wo_cs = {}, {}, {}
    for slot in (3, 1, 2):
        wo_zs[slot].wait_recv()
        wo_xs[slot] = [net.send(wo_part(slot, x), wo_part(slot, x), "x", d) for d in (1, 3)]

    for part in (gk, gv):
        part.swap(2)
    own[2].wait()
    own[3].wait()
    for part in (gk, gv):
        part.ready(1, 2, 3)
    fb2a.wait_recv()
    fb2b.wait_recv()

    rows_f = FB[...].reshape(512, ENC)
    keys = jnp.dot(rows_f, WK[...], preferred_element_type=F32)
    for r in range(4):
        k = keys[:, r * 128 : (r + 1) * 128]
        k = k * lax.rsqrt(jnp.mean(k * k, axis=-1, keepdims=True) + 1e-06) * kg[...].reshape(1, 128)
        KB[r] = k.astype(BF)
    values = jnp.dot(rows_f, WV[...], preferred_element_type=F32)
    for r in range(4):
        VB[r, :, pl.ds(0, 128)] = values[:, r * 128 : (r + 1) * 128].astype(BF)
        VB[r, :, pl.ds(128, 128)] = jnp.ones((512, 128), BF)

    max_take(1, going)
    going = max_send(2)

    sent_assign.wait_recv()
    count = jnp.where(z < 2, tiles[0], tiles[1]) * 256
    col = lax.broadcasted_iota(jnp.int32, (256, 512), 1)
    row = lax.broadcasted_iota(jnp.int32, (256, 512), 0)
    at = ((z % 2) * 4 + ((y + (col >> 7)) & 3)) * 128 + (col & 127)
    chosen = jnp.where((row & 63) < 32, AS2[0:1, 0:1], AS2[0:1, 1:2])
    MK[...] = jnp.where((at < count) & (chosen == z // 2), 1.0, 0.0)

    for copy in qs:
        copy.wait_recv()
    ats = []
    lane_w = lax.broadcasted_iota(jnp.int32, (256, 128), 1)
    for r in (2, 1, 3, 0):
        dens = []
        for h in range(2):
            cols = pl.ds(h * 128, 128)
            scores = lax.dot_general(
                QB[r, :, cols], KB[r], (((1,), (1,)), ((), ())), preferred_element_type=F32
            )
            weights = (jnp.exp(scores * (128**-0.5)) * MK[...]).astype(BF)
            both = jnp.dot(weights, VB[r], preferred_element_type=F32)
            AN[r, :, cols] = both[:, :128].astype(BF)
            dens.append(both[:, 128:])
        packed = jnp.where(lane_w == 0, dens[0], jnp.where(lane_w == 1, dens[1], 0.0))
        AD[r] = packed.T[0:8, :]
        ats.append(net.send(AN.at[r], AT.at[(4 - r) % 4], 1, r))
        ats.append(net.send(AD.at[r], ADT.at[(4 - r) % 4], 1, r))

    for slot in (3, 1, 2):
        if slot == 1:
            wo_xs[slot][1].wait_recv()
            wo_fs[slot] = net.send(wo_part(slot, right), wo_part(slot, right), "x", 3)
        else:
            wo_xs[slot][0].wait_recv()
            wo_fs[slot] = net.send(wo_part(slot, left), wo_part(slot, left), "x", 1)
    for slot in (3, 1, 2):
        wo_xs[slot][0 if slot == 1 else 1].wait_recv()
        wo_fs[slot].wait_recv()
        wo_cs[slot] = net.send(wo_half(slot), wo_half(slot), "c", 1)

    max_take(2, going)
    going = max_send(3)

    for copy in ats:
        copy.wait_recv()
    DN[...] = jnp.ones_like(DN)
    DN[pl.ds(0, 8), :] = ADT[0] + ADT[1] + ADT[2] + ADT[3]
    den = DN[...].T
    for h in range(2):
        cols = pl.ds(h * 128, 128)
        num = AT[0, :, cols].astype(F32) + AT[1, :, cols].astype(F32)
        num = num + AT[2, :, cols].astype(F32) + AT[3, :, cols].astype(F32)
        G[:, cols] = (num / den[:, h : h + 1]).astype(BF)
    gs = [net.send(G.at[:, pl.ds(0, 256)], G.at[:, pl.ds((4 - d) * 256, 256)], "z", d) for d in (1, 3, 2)]

    own[4].wait()
    for slot in (1, 2, 3):
        wo_cs[slot].wait_recv()
    for copy in gs:
        copy.wait_recv()

    olo, ohi = pl.ds(0, 1024), pl.ds(1024, 1024)
    OF[...] = jnp.dot(G[...], WO[:, olo], preferred_element_type=F32)
    OS[0, :, olo] = OF[pl.ds(128, 64), :].astype(BF)
    ox0 = net.send(OS.at[0, :, olo], OX.at[0], "y", 1)
    OS[2, :, olo] = OF[pl.ds(192, 64), :].astype(BF)
    out_lo = OF[pl.ds(0, 64), :]
    oplus = OF[pl.ds(64, 64), :]
    OF[...] = jnp.dot(G[...], WO[:, ohi], preferred_element_type=F32)
    OS[0, :, ohi] = OF[pl.ds(128, 64), :].astype(BF)
    ox1 = net.send(OS.at[0, :, ohi], OX.at[1], "y", 3)
    OS[1, :, ohi] = OF[pl.ds(64, 64), :].astype(BF)
    ox0.wait_recv()
    OS[1, :, olo] = (oplus + OX[0].astype(F32)).astype(BF)
    oy0 = net.send(OS.at[1], OY.at[0], "y", 1)
    ox1.wait_recv()
    OS[2, :, ohi] = (OF[pl.ds(192, 64), :] + OX[1].astype(F32)).astype(BF)
    oy1 = net.send(OS.at[2], OY.at[1], "y", 3)
    max_take(3, going)
    going = max_send(4)
    oy0.wait_recv()
    oy1.wait_recv()
    FS[:, olo] = (out_lo + OY[0, :, olo].astype(F32) + OY[1, :, olo].astype(F32)).astype(BF)
    FS[:, ohi] = (OF[pl.ds(0, 64), :] + OY[0, :, ohi].astype(F32) + OY[1, :, ohi].astype(F32)).astype(BF)
    fs = {}
    for d in (2, 1, 3):
        fs[4 - d] = net.send(FS.at[rows_of(((z + d) % 4) * 16, 16)], MX.at[4 - d], "z", d)
    max_take(4, going)
    amax_out[:, 0:1] = CUR[5][0:4, 0:1]
    amax_out[:, pl.ds(1, 15)] = hist[:, pl.ds(0, 15)]
    strength = jnp.tanh(jnp.full((1, 128), gate[0], F32))[:, 0:1]
    for r in (0, 1, 3, 2):
        cols = rows_of(((z + r) % 4) * 2048, 2048, 128)
        if r:
            fs[r].wait_recv()
            total = MX[r].astype(F32)
        else:
            total = FS[rows_of(z * 16, 16), :].astype(F32)
        mixed_out[:, cols] = (text[:, cols].astype(F32) + strength * total).astype(BF)
    net.finish()


def hand_over(mixed, feat, amax, mixed_out, feat_out, amax_out):
    mixed_out[...] = mixed[...]
    feat_out[...] = feat[...]
    amax_out[...] = amax[...]


def local(
    image, text, ln_gain, ln_bias, w_up, b_up, w_down, b_down, tile_count, assign,
    w_key, w_value, in_gain, w_query, q_gain, k_gain, w_out, attn_gate, amax_hist,
):
    vm = pl.BlockSpec(memory_space=pltpu.VMEM)
    sm = pl.BlockSpec(memory_space=pltpu.SMEM)
    hbm = pl.BlockSpec(memory_space=pl.ANY)
    outs = pl.pallas_call(
        kernel,
        out_shape=(
            jax.ShapeDtypeStruct((16, D), BF),
            jax.ShapeDtypeStruct((ROWS, ENC), BF),
            jax.ShapeDtypeStruct((4, 16), F32),
        ),
        in_specs=[vm] * 6 + [sm] * 2 + [vm] * 3 + [sm, vm] + [hbm] * 6,
        out_specs=(vm, vm, vm),
        scratch_shapes=[
            pltpu.VMEM((4 * SH, ENC), BF),
            pltpu.VMEM((4 * SH, ENC), BF),
            pltpu.VMEM((ENC, 512), BF),
            pltpu.VMEM((ENC, 512), BF),
            pltpu.VMEM((1024, 2048), BF),
            pltpu.VMEM((D, 256), BF),
            pltpu.VMEM((4, 8, 384), F32),
            pltpu.VMEM((4, ROWS, ENC), BF),
            pltpu.VMEM((512, 4 * SH), BF),
            pltpu.VMEM((1, 640), F32),
            pltpu.VMEM((512, 640), F32),
            pltpu.VMEM((3, ROWS, ENC), BF),
            pltpu.VMEM((2, ROWS, 640), BF),
            pltpu.VMEM((2, ROWS, ENC), BF),
            pltpu.VMEM((6, 8, 128), F32),
            pltpu.VMEM((5, 3, 8, 128), F32),
            pltpu.VMEM((256, D), BF),
            pltpu.VMEM((256, 256), F32),
            pltpu.VMEM((256, 256), BF),
            pltpu.VMEM((4, 256, 256), BF),
            pltpu.VMEM((8, 128), jnp.int32),
            pltpu.VMEM((4, ROWS, ENC), BF),
            pltpu.VMEM((4, 512, 128), BF),
            pltpu.VMEM((4, 512, 256), BF),
            pltpu.VMEM((256, 512), F32),
            pltpu.VMEM((8, 128), jnp.int32),
            pltpu.VMEM((4, 256, 256), BF),
            pltpu.VMEM((4, 8, 256), F32),
            pltpu.VMEM((4, 256, 256), BF),
            pltpu.VMEM((4, 8, 256), F32),
            pltpu.VMEM((128, 256), F32),
            pltpu.VMEM((256, 1024), BF),
            pltpu.VMEM((256, 1024), F32),
            pltpu.VMEM((3, 64, 2048), BF),
            pltpu.VMEM((2, 64, 1024), BF),
            pltpu.VMEM((2, 64, 2048), BF),
            pltpu.VMEM((64, 2048), BF),
            pltpu.VMEM((4, 16, 2048), BF),
            pltpu.SemaphoreType.DMA((8,)),
            pltpu.SemaphoreType.DMA((NSEM,)),
            pltpu.SemaphoreType.DMA((NSEM,)),
        ],
        compiler_params=pltpu.CompilerParams(
            collective_id=0, has_side_effects=True, vmem_limit_bytes=60 << 20
        ),
        name="block",
    )(
        image, text, ln_gain, ln_bias, b_up, b_down, tile_count, assign, in_gain, q_gain, k_gain,
        attn_gate, amax_hist.T, w_up.T, w_down, w_key, w_value, w_query, w_out,
    )
    mixed, feat, amax = pl.pallas_call(
        hand_over,
        out_shape=[jax.ShapeDtypeStruct(o.shape, o.dtype) for o in outs],
        in_specs=[vm] * 3,
        out_specs=[vm] * 3,
        name="hand_over",
    )(*outs)
    return mixed, feat, amax.T


def solution(mesh):
    rows = P(("grp", "tp"), None)
    in_specs = (
        rows, rows, P(), P(), P(None, "tp"), P("tp"), P("tp", None), P(), P("grp"), P("grp"),
        P(None, "tp"), P(None, "tp"), P(), P(None, "tp"), P(), P(), P("tp", None), P(), P(),
    )
    return jax.shard_map(local, mesh=mesh, in_specs=in_specs, out_specs=(rows, rows, P()), check_vma=False)
```

```python
import functools

import jax
import jax.numpy as jnp
from jax import lax
from jax.experimental import pallas as pl
from jax.experimental.pallas import tpu as pltpu
from jax.sharding import PartitionSpec as P

MESH = pl.DeviceIdType.MESH
BF = jnp.bfloat16
F32 = jnp.float32
D = 8192
ROWS = 128
ENC = 1280
SH = 320
NSEM = 160


class Net:
    def __init__(self, ssem, rsem):
        self.ssem, self.rsem, self.used, self.sent = ssem, rsem, 0, []
        g, t = lax.axis_index("grp"), lax.axis_index("tp")
        self.g, self.t = g, t
        self.core, self.x, self.zl = g % 2, (g // 2) % 4, g // 8
        self.y, self.z = t % 4, t // 4

    def peer(self, axis, d):
        if axis == "y":
            return (self.g, self.z * 4 + (self.y + d) % 4)
        if axis == "z":
            return (self.g, ((self.z + d) % 4) * 4 + self.y)
        if axis == "x":
            return ((self.zl * 4 + (self.x + d) % 4) * 2 + self.core, self.t)
        if axis == "l":
            return ((self.g + 8) % 16, self.t)
        if axis == "c":
            return (self.g + 1 - 2 * self.core, self.t)
        return ((self.g + axis) % 16, ((self.z + d) % 4) * 4 + self.y)

    def barrier(self, peers):
        sem = pltpu.get_barrier_semaphore()
        for axis, d in peers:
            pl.semaphore_signal(sem, inc=1, device_id=self.peer(axis, d), device_id_type=MESH)
        pl.semaphore_wait(sem, len(peers))

    def send(self, src, dst, axis, d):
        k = self.used
        self.used += 1
        copy = pltpu.make_async_remote_copy(
            src_ref=src,
            dst_ref=dst,
            send_sem=self.ssem.at[k],
            recv_sem=self.rsem.at[k],
            device_id=self.peer(axis, d),
            device_id_type=MESH,
        )
        copy.start()
        self.sent.append(copy)
        return copy

    def finish(self):
        for copy in self.sent:
            copy.wait_send()


def rows_of(start, size, unit=16):
    return pl.ds(pl.multiple_of(start, unit), size)


def total_max(values):
    return jnp.max(jnp.max(values, axis=0, keepdims=True), axis=1, keepdims=True)


def kernel(
    image, text, lng, lnb, bup, bdown, tiles, assign, ing, qg, kg, gate, hist,
    wup, wdown, wkey, wvalue, wquery, wout,
    mixed_out, feat_out, amax_out,
    WU, WD, WK, WV, WO, WQ, BU, NB, HB, HM, PF, PS, RX, RY, CUR, CR,
    T, QA, QO, QB, AS, FB, KB, VB, MK, AS2, AN, AD, AT, ADT, DN, G, OF, OS, OX, OY, FS, MX,
    lsem, ssem, rsem,
):
    net = Net(ssem, rsem)
    x, y, z, c = net.x, net.y, net.z, net.core
    net.barrier(
        [("y", 1), ("y", 2), ("y", 3), ("z", 1), ("z", 2), ("z", 3), ("x", 1), ("x", 2), ("x", 3)]
        + [("c", 1), ("l", 1)]
        + [(by, d) for by in (1, -1) for d in range(4)]
    )

    def up_part(ref, slot, at):
        return ref.at[rows_of(slot * SH + at * 80, 80), rows_of(c * 640, 640, 128)]

    def up_half(ref, slot):
        return ref.at[pl.ds(slot * SH, SH), rows_of(c * 640, 640, 128)]

    def kv_part(ref, slot, at):
        return ref.at[rows_of(c * 640 + at * 160, 160), pl.ds(slot * 128, 128)]

    def kv_half(ref, slot):
        return ref.at[rows_of(c * 640, 640), pl.ds(slot * 128, 128)]

    def wo_part(slot, at):
        return WO.at[rows_of(slot * 256 + at * 64, 64), rows_of(c * 1024, 1024, 128)]

    def wo_half(slot):
        return WO.at[pl.ds(slot * 256, 256), rows_of(c * 1024, 1024, 128)]

    left, right = (x + 3) % 4, (x + 1) % 4

    class Gather:
        def __init__(self, ref, source, part, half, forward):
            self.ref, self.part, self.half, self.forward = ref, part, half, forward
            self.zs, self.xs, self.fs, self.cs = {}, {}, {}, {}
            self.zs[3] = net.send(source, part(ref, 3, x), "z", 1)
            self.zs[1] = net.send(source, part(ref, 1, x), "z", 3)

        def z_got(self, slot):
            self.zs[slot].wait_recv()
            if slot == (3 if self.forward > 0 else 1):
                d = 1 if self.forward > 0 else 3
                self.zs[2] = net.send(self.part(self.ref, slot, x), self.part(self.ref, 2, x), "z", d)
            mine = self.part(self.ref, slot, x)
            self.xs[slot] = [net.send(mine, mine, "x", d) for d in (1, 3)]

        def x_got(self, slot):
            if self.forward > 0:
                self.xs[slot][0].wait_recv()
                other = self.part(self.ref, slot, left)
                self.fs[slot] = net.send(other, other, "x", 1)
            else:
                self.xs[slot][1].wait_recv()
                other = self.part(self.ref, slot, right)
                self.fs[slot] = net.send(other, other, "x", 3)

        def swap(self, slot):
            self.xs[slot][1 if self.forward > 0 else 0].wait_recv()
            self.fs[slot].wait_recv()
            mine = self.half(self.ref, slot)
            self.cs[slot] = net.send(mine, mine, "c", 1)

        def ready(self, *slots):
            for slot in slots:
                self.cs[slot].wait_recv()

    own = [
        pltpu.make_async_copy(wup, WU.at[pl.ds(0, SH)], lsem.at[0]),
        pltpu.make_async_copy(wdown, WD.at[pl.ds(0, SH)], lsem.at[1]),
        pltpu.make_async_copy(wkey, WK.at[:, pl.ds(0, 128)], lsem.at[2]),
        pltpu.make_async_copy(wvalue, WV.at[:, pl.ds(0, 128)], lsem.at[3]),
        pltpu.make_async_copy(
            wout.at[:, rows_of(z * 2048, 2048, 128)], WO.at[pl.ds(0, 256)], lsem.at[4]
        ),
        pltpu.make_async_copy(wquery, WQ, lsem.at[5]),
    ]
    for copy in own:
        copy.start()

    mine = (rows_of(x * 80, 80), rows_of(c * 640, 640, 128))
    gu = Gather(WU, wup.at[mine], up_part, up_half, 1)
    gd = Gather(WD, wdown.at[mine], up_part, up_half, -1)
    BU[0, 0:1, pl.ds(0, SH)] = bup[...].reshape(1, SH)
    zb = [net.send(BU.at[0], BU.at[(4 - d) % 4], "z", d) for d in (1, 2, 3)]

    limits = jnp.max(hist[...], axis=1, keepdims=True)
    lim = [limits[i : i + 1, :] for i in range(4)]

    image_f = image[...].astype(F32)
    centred = image_f - jnp.mean(image_f, axis=-1, keepdims=True)
    spread = jnp.mean(centred * centred, axis=-1, keepdims=True)
    normed = centred * lax.rsqrt(spread + 1e-05) * lng[...].reshape(1, ENC) + lnb[...].reshape(1, ENC)
    cur0 = total_max(jnp.abs(normed))
    NB[0] = jnp.clip(normed, -lim[0], lim[0]).astype(BF)
    nb3 = net.send(NB.at[0], NB.at[3], "y", 1)
    nb1 = net.send(NB.at[0], NB.at[1], "y", 3)

    text_f = text[...].astype(F32)
    tnormed = text_f * lax.rsqrt(jnp.mean(text_f * text_f, axis=-1, keepdims=True) + 1e-05)
    tnormed = tnormed * ing[...].reshape(1, D)
    cur3 = total_max(jnp.abs(tnormed))
    tlo, thi = pl.ds(0, D // 2), pl.ds(D // 2, D // 2)

    def tb(ry, zi):
        return rows_of(ry * 64 + zi * 16, 16)

    T[tb(0, z), :] = jnp.clip(tnormed, -lim[3], lim[3]).astype(BF)

    lane = lax.broadcasted_iota(jnp.int32, (8, 128), 1)
    AS[...] = jnp.where(lane == 0, assign[0], assign[1])
    sent_assign = net.send(AS, AS2, -1, 0)

    gu.z_got(3)
    gu.z_got(1)
    gd.z_got(1)
    gd.z_got(3)

    zl, zr = (z + 3) % 4, (z + 1) % 4
    tz3 = net.send(T.at[tb(0, z)], T.at[tb(0, z)], "z", 1)
    tz1 = net.send(T.at[tb(0, z)], T.at[tb(0, z)], "z", 3)

    lo, hi = pl.ds(0, 640), pl.ds(640, 640)
    nb3.wait_recv()
    nb2a = net.send(NB.at[3, :, lo], NB.at[2, :, lo], "y", 1)
    nb1.wait_recv()
    nb2b = net.send(NB.at[1, :, hi], NB.at[2, :, hi], "y", 3)

    class TextRing:
        def __init__(self, zi):
            self.zi = zi
            own_block = T.at[tb(0, zi)]
            self.a3 = net.send(own_block, T.at[tb(3, zi)], "y", 1)
            self.a1 = net.send(own_block, T.at[tb(1, zi)], "y", 3)

        def relay(self):
            self.a3.wait_recv()
            self.f = [net.send(T.at[tb(3, self.zi), tlo], T.at[tb(2, self.zi), tlo], "y", 1)]
            self.a1.wait_recv()
            self.f.append(net.send(T.at[tb(1, self.zi), thi], T.at[tb(2, self.zi), thi], "y", 3))

        def done(self):
            for copy in self.f:
                copy.wait_recv()

    rings = [TextRing(z)]

    gu.x_got(3)
    gu.z_got(2)
    gu.x_got(1)
    gd.x_got(1)
    gd.z_got(2)
    gu.swap(1)
    gd.x_got(3)
    gu.x_got(2)
    gu.swap(3)
    gk = Gather(WK, wkey.at[rows_of(c * 640 + x * 160, 160), :], kv_part, kv_half, 1)
    gv = Gather(WV, wvalue.at[rows_of(c * 640 + x * 160, 160), :], kv_part, kv_half, -1)
    rings[0].relay()
    nb2a.wait_recv()
    nb2b.wait_recv()
    own[0].wait()
    for copy in zb:
        copy.wait_recv()
    gd.x_got(2)
    gu.swap(2)
    gu.ready(1)
    gd.swap(1)
    gd.swap(3)

    tz3.wait_recv()
    tz2a = net.send(T.at[tb(0, zl), tlo], T.at[tb(0, zl), tlo], "z", 1)
    rings.append(TextRing(zl))
    tz1.wait_recv()
    tz2b = net.send(T.at[tb(0, zr), thi], T.at[tb(0, zr), thi], "z", 3)
    rings.append(TextRing(zr))
    HM[...] = jnp.zeros_like(HM)

    def up(pair):
        units = pl.ds(pair * 640, 640)
        bias = jnp.concatenate([BU[2 * pair][0:1, :SH], BU[2 * pair + 1][0:1, :SH]], axis=1)

        def step(i, carry):
            rows = rows_of(i * 256, 256)
            pre = lax.dot_general(
                NB[pl.ds(i * 2, 2)].reshape(256, ENC), WU[units, :], (((1,), (1,)), ((), ())),
                preferred_element_type=F32,
            )
            pre = pre + bias
            hidden = 0.5 * pre * (1.0 + lax.erf(pre * (0.5**0.5)))
            HM[...] = jnp.maximum(HM[...], jnp.max(jnp.abs(hidden), axis=0, keepdims=True))
            HB[rows, units] = jnp.clip(hidden, -lim[1], lim[1]).astype(BF)
            return carry

        lax.fori_loop(0, 2, step, 0)

    up(0)
    gd.swap(2)
    gu.ready(2, 3)
    tz2a.wait_recv()
    tz2b.wait_recv()
    zo = (z + 2) % 4
    rings.append(TextRing(zo))
    up(1)
    own[1].wait()
    gd.ready(1, 2, 3)

    def down(cols):
        PF[...] = jnp.dot(HB[...], WD[:, cols], preferred_element_type=F32)

    down(lo)
    PS[0, :, lo] = PF[pl.ds(256, 128), :].astype(BF)
    rx0 = net.send(PS.at[0, :, lo], RX.at[0], "y", 1)
    PS[2, :, lo] = PF[pl.ds(384, 128), :].astype(BF)
    OWN0 = image[:, lo].astype(F32) + bdown[lo].reshape(1, 640) + PF[pl.ds(0, 128), :]
    plus_lo = PF[pl.ds(128, 128), :]
    down(hi)
    PS[0, :, hi] = PF[pl.ds(256, 128), :].astype(BF)
    rx1 = net.send(PS.at[0, :, hi], RX.at[1], "y", 3)
    PS[1, :, hi] = PF[pl.ds(128, 128), :].astype(BF)
    rx0.wait_recv()
    PS[1, :, lo] = (plus_lo + RX[0].astype(F32)).astype(BF)
    ry0 = net.send(PS.at[1], RY.at[0], "y", 1)
    rx1.wait_recv()
    PS[2, :, hi] = (PF[pl.ds(384, 128), :] + RX[1].astype(F32)).astype(BF)
    ry1 = net.send(PS.at[2], RY.at[1], "y", 3)

    rings[1].relay()
    rings[2].relay()
    for part in (gk, gv):
        part.z_got(3)
        part.z_got(1)
    wo_zs = {}
    for d in (1, 3, 2):
        cut = rows_of(((z + d) % 4) * 2048 + c * 1024, 1024, 128)
        wo_zs[4 - d] = net.send(wout.at[rows_of(x * 64, 64), cut], wo_part(4 - d, x), "z", d)

    ry0.wait_recv()
    ry1.wait_recv()
    feat_lo = OWN0 + RY[0, :, lo].astype(F32) + RY[1, :, lo].astype(F32)
    feat_hi = image[:, hi].astype(F32) + bdown[hi].reshape(1, 640) + PF[pl.ds(0, 128), :]
    feat_hi = feat_hi + RY[0, :, hi].astype(F32) + RY[1, :, hi].astype(F32)
    cur2 = jnp.maximum(total_max(jnp.abs(feat_lo)), total_max(jnp.abs(feat_hi)))
    FB[0, :, lo] = jnp.clip(feat_lo, -lim[2], lim[2]).astype(BF)
    FB[0, :, hi] = jnp.clip(feat_hi, -lim[2], lim[2]).astype(BF)
    fb3 = net.send(FB.at[0], FB.at[3], "y", 1)
    fb1 = net.send(FB.at[0], FB.at[1], "y", 3)
    feat_out[...] = FB[0]

    cur1 = total_max(HM[...])
    line = lax.broadcasted_iota(jnp.int32, (8, 128), 0)
    cur = jnp.where(line == 0, cur0, 0.0) + jnp.where(line == 1, cur1, 0.0)
    cur = cur + jnp.where(line == 2, cur2, 0.0) + jnp.where(line == 3, cur3, 0.0)
    CUR[0] = cur
    stages = (("c", (1,)), ("y", (1, 2, 3)), ("x", (1, 2, 3)), ("z", (1, 2, 3)), ("l", (1,)))

    def max_send(i):
        axis, ds = stages[i]
        return [net.send(CUR.at[i], CR.at[i, j], axis, d) for j, d in enumerate(ds)]

    def max_take(i, copies):
        value = CUR[i]
        for j, copy in enumerate(copies):
            copy.wait_recv()
            value = jnp.maximum(value, CR[i, j])
        CUR[i + 1] = value

    going = max_send(0)

    for part in (gk, gv):
        part.z_got(2)
        part.x_got(3)
        part.x_got(1)

    fb3.wait_recv()
    fb2a = net.send(FB.at[3, :, lo], FB.at[2, :, lo], "y", 1)
    fb1.wait_recv()
    fb2b = net.send(FB.at[1, :, hi], FB.at[2, :, hi], "y", 3)
    max_take(0, going)
    going = max_send(1)

    for part in (gk, gv):
        part.x_got(2)
        part.swap(1)
        part.swap(3)

    rings[3].relay()
    for ring in rings:
        ring.done()
    own[5].wait()
    QA[...] = jnp.zeros_like(QA)

    def query_step(i, carry):
        span = rows_of(i * 1024, 1024, 128)
        QA[...] += jnp.dot(T[:, span], WQ[span, :], preferred_element_type=F32)
        return carry

    lax.fori_loop(0, D // 1024, query_step, 0)
    for h in range(2):
        cols = pl.ds(h * 128, 128)
        q = QA[:, cols]
        q = q * lax.rsqrt(jnp.mean(q * q, axis=-1, keepdims=True) + 1e-06) * qg[...].reshape(1, 128)
        QO[:, cols] = q.astype(BF)
    qs = [net.send(QO, QB.at[(4 - d) % 4], -1, d) for d in range(4)]

    wo_xs, wo_fs, wo_cs = {}, {}, {}
    for slot in (3, 1, 2):
        wo_zs[slot].wait_recv()
        wo_xs[slot] = [net.send(wo_part(slot, x), wo_part(slot, x), "x", d) for d in (1, 3)]

    for part in (gk, gv):
        part.swap(2)
    own[2].wait()
    own[3].wait()
    for part in (gk, gv):
        part.ready(1, 2, 3)
    fb2a.wait_recv()
    fb2b.wait_recv()

    rows_f = FB[...].reshape(512, ENC)
    keys = jnp.dot(rows_f, WK[...], preferred_element_type=F32)
    for r in range(4):
        k = keys[:, r * 128 : (r + 1) * 128]
        k = k * lax.rsqrt(jnp.mean(k * k, axis=-1, keepdims=True) + 1e-06) * kg[...].reshape(1, 128)
        KB[r] = k.astype(BF)
    values = jnp.dot(rows_f, WV[...], preferred_element_type=F32)
    for r in range(4):
        VB[r, :, pl.ds(0, 128)] = values[:, r * 128 : (r + 1) * 128].astype(BF)
        VB[r, :, pl.ds(128, 128)] = jnp.ones((512, 128), BF)

    max_take(1, going)
    going = max_send(2)

    sent_assign.wait_recv()
    count = jnp.where(z < 2, tiles[0], tiles[1]) * 256
    col = lax.broadcasted_iota(jnp.int32, (256, 512), 1)
    row = lax.broadcasted_iota(jnp.int32, (256, 512), 0)
    at = ((z % 2) * 4 + ((y + (col >> 7)) & 3)) * 128 + (col & 127)
    chosen = jnp.where((row & 63) < 32, AS2[0:1, 0:1], AS2[0:1, 1:2])
    MK[...] = jnp.where((at < count) & (chosen == z // 2), 1.0, 0.0)

    for copy in qs:
        copy.wait_recv()
    ats = []
    lane_w = lax.broadcasted_iota(jnp.int32, (256, 128), 1)
    for r in (2, 1, 3, 0):
        dens = []
        for h in range(2):
            cols = pl.ds(h * 128, 128)
            scores = lax.dot_general(
                QB[r, :, cols], KB[r], (((1,), (1,)), ((), ())), preferred_element_type=F32
            )
            weights = (jnp.exp(scores * (128**-0.5)) * MK[...]).astype(BF)
            both = jnp.dot(weights, VB[r], preferred_element_type=F32)
            AN[r, :, cols] = both[:, :128].astype(BF)
            dens.append(both[:, 128:])
        packed = jnp.where(lane_w == 0, dens[0], jnp.where(lane_w == 1, dens[1], 0.0))
        AD[r] = packed.T[0:8, :]
        ats.append(net.send(AN.at[r], AT.at[(4 - r) % 4], 1, r))
        ats.append(net.send(AD.at[r], ADT.at[(4 - r) % 4], 1, r))

    for slot in (3, 1, 2):
        if slot == 1:
            wo_xs[slot][1].wait_recv()
            wo_fs[slot] = net.send(wo_part(slot, right), wo_part(slot, right), "x", 3)
        else:
            wo_xs[slot][0].wait_recv()
            wo_fs[slot] = net.send(wo_part(slot, left), wo_part(slot, left), "x", 1)
    for slot in (3, 1, 2):
        wo_xs[slot][0 if slot == 1 else 1].wait_recv()
        wo_fs[slot].wait_recv()
        wo_cs[slot] = net.send(wo_half(slot), wo_half(slot), "c", 1)

    max_take(2, going)
    going = max_send(3)

    for copy in ats:
        copy.wait_recv()
    DN[...] = jnp.ones_like(DN)
    DN[pl.ds(0, 8), :] = ADT[0] + ADT[1] + ADT[2] + ADT[3]
    den = DN[...].T
    for h in range(2):
        cols = pl.ds(h * 128, 128)
        num = AT[0, :, cols].astype(F32) + AT[1, :, cols].astype(F32)
        num = num + AT[2, :, cols].astype(F32) + AT[3, :, cols].astype(F32)
        G[:, cols] = (num / den[:, h : h + 1]).astype(BF)
    gs = [net.send(G.at[:, pl.ds(0, 256)], G.at[:, pl.ds((4 - d) * 256, 256)], "z", d) for d in (1, 3, 2)]

    own[4].wait()
    for slot in (1, 2, 3):
        wo_cs[slot].wait_recv()
    for copy in gs:
        copy.wait_recv()

    olo, ohi = pl.ds(0, 1024), pl.ds(1024, 1024)
    OF[...] = jnp.dot(G[...], WO[:, olo], preferred_element_type=F32)
    OS[0, :, olo] = OF[pl.ds(128, 64), :].astype(BF)
    ox0 = net.send(OS.at[0, :, olo], OX.at[0], "y", 1)
    OS[2, :, olo] = OF[pl.ds(192, 64), :].astype(BF)
    out_lo = OF[pl.ds(0, 64), :]
    oplus = OF[pl.ds(64, 64), :]
    OF[...] = jnp.dot(G[...], WO[:, ohi], preferred_element_type=F32)
    OS[0, :, ohi] = OF[pl.ds(128, 64), :].astype(BF)
    ox1 = net.send(OS.at[0, :, ohi], OX.at[1], "y", 3)
    OS[1, :, ohi] = OF[pl.ds(64, 64), :].astype(BF)
    ox0.wait_recv()
    OS[1, :, olo] = (oplus + OX[0].astype(F32)).astype(BF)
    oy0 = net.send(OS.at[1], OY.at[0], "y", 1)
    ox1.wait_recv()
    OS[2, :, ohi] = (OF[pl.ds(192, 64), :] + OX[1].astype(F32)).astype(BF)
    oy1 = net.send(OS.at[2], OY.at[1], "y", 3)
    max_take(3, going)
    going = max_send(4)
    oy0.wait_recv()
    oy1.wait_recv()
    FS[:, olo] = (out_lo + OY[0, :, olo].astype(F32) + OY[1, :, olo].astype(F32)).astype(BF)
    FS[:, ohi] = (OF[pl.ds(0, 64), :] + OY[0, :, ohi].astype(F32) + OY[1, :, ohi].astype(F32)).astype(BF)
    fs = {}
    for d in (2, 1, 3):
        fs[4 - d] = net.send(FS.at[rows_of(((z + d) % 4) * 16, 16)], MX.at[4 - d], "z", d)
    max_take(4, going)
    amax_out[:, 0:1] = CUR[5][0:4, 0:1]
    amax_out[:, pl.ds(1, 15)] = hist[:, pl.ds(0, 15)]
    strength = jnp.tanh(jnp.full((1, 128), gate[0], F32))[:, 0:1]
    for r in (0, 1, 3, 2):
        cols = rows_of(((z + r) % 4) * 2048, 2048, 128)
        if r:
            fs[r].wait_recv()
            total = MX[r].astype(F32)
        else:
            total = FS[rows_of(z * 16, 16), :].astype(F32)
        mixed_out[:, cols] = (text[:, cols].astype(F32) + strength * total).astype(BF)
    net.finish()


def hand_over(mixed, feat, amax, mixed_out, feat_out, amax_out):
    mixed_out[...] = mixed[...]
    feat_out[...] = feat[...]
    amax_out[...] = amax[...]


def local(
    image, text, ln_gain, ln_bias, w_up, b_up, w_down, b_down, tile_count, assign,
    w_key, w_value, in_gain, w_query, q_gain, k_gain, w_out, attn_gate, amax_hist,
):
    vm = pl.BlockSpec(memory_space=pltpu.VMEM)
    sm = pl.BlockSpec(memory_space=pltpu.SMEM)
    hbm = pl.BlockSpec(memory_space=pl.ANY)
    outs = pl.pallas_call(
        kernel,
        out_shape=(
            jax.ShapeDtypeStruct((16, D), BF),
            jax.ShapeDtypeStruct((ROWS, ENC), BF),
            jax.ShapeDtypeStruct((4, 16), F32),
        ),
        in_specs=[vm] * 6 + [sm] * 2 + [vm] * 3 + [sm, vm] + [hbm] * 6,
        out_specs=(vm, vm, vm),
        scratch_shapes=[
            pltpu.VMEM((4 * SH, ENC), BF),
            pltpu.VMEM((4 * SH, ENC), BF),
            pltpu.VMEM((ENC, 512), BF),
            pltpu.VMEM((ENC, 512), BF),
            pltpu.VMEM((1024, 2048), BF),
            pltpu.VMEM((D, 256), BF),
            pltpu.VMEM((4, 8, 384), F32),
            pltpu.VMEM((4, ROWS, ENC), BF),
            pltpu.VMEM((512, 4 * SH), BF),
            pltpu.VMEM((1, 640), F32),
            pltpu.VMEM((512, 640), F32),
            pltpu.VMEM((3, ROWS, ENC), BF),
            pltpu.VMEM((2, ROWS, 640), BF),
            pltpu.VMEM((2, ROWS, ENC), BF),
            pltpu.VMEM((6, 8, 128), F32),
            pltpu.VMEM((5, 3, 8, 128), F32),
            pltpu.VMEM((256, D), BF),
            pltpu.VMEM((256, 256), F32),
            pltpu.VMEM((256, 256), BF),
            pltpu.VMEM((4, 256, 256), BF),
            pltpu.VMEM((8, 128), jnp.int32),
            pltpu.VMEM((4, ROWS, ENC), BF),
            pltpu.VMEM((4, 512, 128), BF),
            pltpu.VMEM((4, 512, 256), BF),
            pltpu.VMEM((256, 512), F32),
            pltpu.VMEM((8, 128), jnp.int32),
            pltpu.VMEM((4, 256, 256), BF),
            pltpu.VMEM((4, 8, 256), F32),
            pltpu.VMEM((4, 256, 256), BF),
            pltpu.VMEM((4, 8, 256), F32),
            pltpu.VMEM((128, 256), F32),
            pltpu.VMEM((256, 1024), BF),
            pltpu.VMEM((256, 1024), F32),
            pltpu.VMEM((3, 64, 2048), BF),
            pltpu.VMEM((2, 64, 1024), BF),
            pltpu.VMEM((2, 64, 2048), BF),
            pltpu.VMEM((64, 2048), BF),
            pltpu.VMEM((4, 16, 2048), BF),
            pltpu.SemaphoreType.DMA((8,)),
            pltpu.SemaphoreType.DMA((NSEM,)),
            pltpu.SemaphoreType.DMA((NSEM,)),
        ],
        compiler_params=pltpu.CompilerParams(
            collective_id=0, has_side_effects=True, vmem_limit_bytes=60 << 20
        ),
        name="block",
    )(
        image, text, ln_gain, ln_bias, b_up, b_down, tile_count, assign, in_gain, q_gain, k_gain,
        attn_gate, amax_hist.T, w_up.T, w_down, w_key, w_value, w_query, w_out,
    )
    mixed, feat, amax = pl.pallas_call(
        hand_over,
        out_shape=[jax.ShapeDtypeStruct(o.shape, o.dtype) for o in outs],
        in_specs=[vm] * 3,
        out_specs=[vm] * 3,
        name="hand_over",
    )(*outs)
    return mixed, feat, amax.T


def solution(mesh):
    rows = P(("grp", "tp"), None)
    in_specs = (
        rows, rows, P(), P(), P(None, "tp"), P("tp"), P("tp", None), P(), P("grp"), P("grp"),
        P(None, "tp"), P(None, "tp"), P(), P(None, "tp"), P(), P(), P("tp", None), P(), P(),
    )
    return jax.shard_map(local, mesh=mesh, in_specs=in_specs, out_specs=(rows, rows, P()), check_vma=False)
```
